128 devices in a mesh: shot: 4 (over z_lo, core), space: 32 (over y, z_hi, x).
Axes of the slice: x: 4, y: 4, z: 4 (z_hi: 2, z_lo: 2; z = z_hi * 2 + z_lo), core: 2. Of those that a mesh axis runs over, the one named last changes fastest.
Arguments:
- adjoint_state: float32 [4, 9, 512, 64, 128], P('shot', None, 'space'), may hold values from -6 to 6
- forward_velocity: float32 [4, 4, 3, 512, 64, 128], P('shot', None, None, 'space'), may hold values from -6 to 6
- vp: float32 [512, 64, 128], P('space'), may hold values from 1 to 1.8
- shear_ratio: float32 [512, 64, 128], P('space'), may hold values from 0.45 to 0.65
- density: float32 [512, 64, 128], P('space'), may hold values from 1 to 2.5
- residuals: float32 [4, 3, 32768], P('shot', None, 'space'), may hold values from -12 to 12
- owner: int32 [32768, 1], P('space'), may hold values from 0 to 31; in each aligned block of 1024 rows (0 to 1023, 1024 to 2047, ...) at most 128 rows name the same one
- cell: int32 [32768], P('space'), may hold values from 0 to 131071
Outputs:
- adjoint_final: float32 [4, 9, 512, 64, 128], P('shot', None, 'space')
- gradient: float32 [3, 512, 64, 128], P(None, 'space', 'shot')
The draws below stay inside these ranges and needn't reach their ends.
Inputs may be any that keep to these rules, and one draw needn't show every extreme that they name: Among the 1024 channels of one device no owner appears more than 128 times, and some owner appears exactly 128 times.
All inputs are finite; a program needn't handle non-finite values.
Results may differ from the reference program's by a relative error of at most 0.000032.
Values sent between devices are 32-bit elements; how exact they have to be, the bound alone decides.
A program may use at most 128 MiB of HBM per device.

```python
import math
import jax
import jax.numpy as jnp
import numpy as np
from jax import lax

CX = 16
NY = 64
NZ = 128
CH_DEV = 1024
CAP = 128
STEPS = 3
SWEEPS = 2
SHOTS = 4
NX = 512
CH = 32768
N_SPACE = 32


def touch_ends(result, key, least, high):
    longest = result.shape.index(max(result.shape))
    spots = []
    for shift in (0, 1):
        where = [jax.random.randint(jax.random.fold_in(key, axis), (), 0, length) for axis, length in enumerate(result.shape)]
        where[longest] = (where[longest] + shift) % result.shape[longest]
        spots.append(tuple(where))
    return result.at[spots[0]].set(least).at[spots[1]].set(high)


def level_of(rng, dims, cuts, smallest, high):
    def one(dim, parts):
        draws = jax.random.uniform(jax.random.fold_in(jax.random.fold_in(rng, 6), dim), (parts,), jnp.float32, smallest / len(cuts), high / len(cuts))
        return jnp.repeat(jnp.exp(draws), dims[dim] // parts).reshape((-1,) + (1,) * (len(dims) - dim - 1))

    factor_of = one(*cuts[0])
    for cut in cuts[1:]:
        factor_of = factor_of * one(*cut)
    return factor_of


def shared_out(key, own, number, rows, amount, top, bound, skew):
    ranking = jax.random.permutation(key, amount)
    crowded, common = portions_of(amount, rows * top, bound, skew, True), portions_of(amount, rows * top, bound, skew, False)
    places = jnp.arange(amount)

    def named(tallies, turn):
        used = int((tallies > 0).sum())
        fixed = max(1, used // 4)
        shifted = fixed + (places - fixed + turn * (used - fixed)) % max(1, amount - fixed)
        return jnp.zeros((amount,), jnp.int32).at[ranking[jnp.where(places < fixed, places, shifted)]].set(jnp.asarray(tallies, jnp.int32))

    tallies = jnp.where(number % 4 == 0, named(crowded, number // 4), named(common, number - number // 4 - 1))
    mixed = jax.random.permutation(jax.random.fold_in(own, 3), amount)
    giver, sink = mixed[0:amount // 2 * 2:2], mixed[1:amount // 2 * 2:2]
    margin = jnp.minimum(tallies[giver] - 1, bound - tallies[sink]) // 2
    margin = jnp.where((giver == ranking[0]) | (sink == ranking[0]) | (tallies[sink] == 0), 0, jnp.maximum(margin, 0))
    shifted = jax.random.randint(jax.random.fold_in(own, 4), (amount // 2,), 0, 1 << 20) % (margin + 1)
    tallies = tallies.at[giver].add(-shifted).at[sink].add(shifted)
    items = jnp.searchsorted(jnp.cumsum(tallies), jnp.arange(rows * top), side="right").astype(jnp.int32)
    grid = items.reshape(top, rows).T
    grid = grid[jax.random.permutation(jax.random.fold_in(own, 1), rows)]
    turn = jax.random.randint(jax.random.fold_in(own, 2), (rows, 1), 0, top)
    return jnp.take_along_axis(grid, (jnp.arange(top)[None, :] + turn) % top, axis=1)


def portions_of(amount, total, bound, slope, full):
    portions = [(1 << 20) // math.isqrt(rank ** slope) + 1 for rank in range(1, amount + 1)]
    largest = bound if full else min(bound, max(-(-total // amount), total * portions[0] // sum(portions)))
    least = 1 if total - largest >= amount - 1 else 0
    counts, spare = [largest] + [least] * (amount - 1), total - largest - least * (amount - 1)
    while spare > 0:
        movable = [i for i in range(1, amount) if counts[i] < largest] or [i for i in range(1, amount) if counts[i] < bound]
        mass, remaining = sum([portions[i] for i in movable]), spare
        for i in movable:
            more = min(bound - counts[i], max(1, remaining * portions[i] // mass), spare)
            counts[i] = counts[i] + more
            spare = spare - more
    return np.array(counts)


def centred(stream_key, shape, spread, most, split=(), dtype=jnp.bfloat16):
    entries = jax.random.normal(stream_key, shape, jnp.float32) * spread
    if len(split) > 0:
        entries = level_of(stream_key, shape, split, -0.22, 0.18) * entries
    return jnp.clip(entries, min=-most, max=most).astype(dtype)


def setup_inputs(seed: int = 0) -> dict:
    splits = jax.random.split(jax.random.key(seed), 9)
    adjoint_state = centred(splits[0], (SHOTS, 9, NX, NY, NZ), 1.0, 6.0, ((0, 4), (2, 32)), jnp.float32)
    forward_velocity = centred(splits[1], (SHOTS, STEPS + 1, 3, NX, NY, NZ), 1.0, 6.0, ((0, 4), (3, 32)), jnp.float32)
    vp = jnp.clip(1.0 + 0.79999995 * jax.random.uniform(splits[2], (NX, NY, NZ), jnp.float32) ** level_of(splits[2], (NX, NY, NZ), ((0, 32),), -0.2, 0.2), 1.0, 1.8)
    shear_ratio = jnp.clip(0.45 + 0.19999999 * jax.random.uniform(splits[3], (NX, NY, NZ), jnp.float32) ** level_of(splits[3], (NX, NY, NZ), ((0, 32),), -0.2, 0.2), 0.45, 0.65)
    density = jnp.clip(jnp.exp(math.log(2.5) - 0.916290732 * jax.random.uniform(splits[4], (NX, NY, NZ), jnp.float32) ** level_of(splits[4], (NX, NY, NZ), ((0, 32),), -0.2, 0.2)), 1.0, 2.5)
    residuals = centred(splits[5], (SHOTS, STEPS, CH), 2.0, 12.0, ((0, 4), (2, 32)), jnp.float32)
    owner_keys = jax.random.split(jax.random.fold_in(splits[6], 1), CH // CH_DEV)
    owner_turns = jax.random.permutation(jax.random.fold_in(splits[6], 3), CH // CH_DEV)
    owner = jax.vmap(lambda own, number: shared_out(jax.random.fold_in(splits[6], 2), own, number, CH_DEV, N_SPACE, 1, CAP, 2))(owner_keys, owner_turns).reshape((CH, 1))
    cell = touch_ends(jax.random.randint(splits[7], (CH,), 0, CX * NY * NZ), jax.random.fold_in(splits[7], 1), 0, (CX * NY * NZ) - 1).astype(jnp.int32)
    return dict(adjoint_state=adjoint_state, forward_velocity=forward_velocity, vp=vp, shear_ratio=shear_ratio, density=density, residuals=residuals, owner=owner, cell=cell)


COURANT = 0.3
KAPPA = 0.15


def plus(f, axis):
    widths = [(0, 0)] * f.ndim
    widths[axis] = (0, 1)
    padded = jnp.pad(f, widths)
    return lax.slice_in_dim(padded, 1, f.shape[axis] + 1, axis=axis) - f


def minus(f, axis):
    widths = [(0, 0)] * f.ndim
    widths[axis] = (1, 0)
    padded = jnp.pad(f, widths)
    return f - lax.slice_in_dim(padded, 0, f.shape[axis], axis=axis)


def advance(fields, buoy, lam, shear):
    vx, vy, vz, sxx, syy, szz, sxy, sxz, syz = fields
    vx = vx + COURANT * buoy * (plus(sxx, 0) + minus(sxy, 1) + minus(sxz, 2))
    vy = vy + COURANT * buoy * (minus(sxy, 0) + plus(syy, 1) + minus(syz, 2))
    vz = vz + COURANT * buoy * (minus(sxz, 0) + minus(syz, 1) + plus(szz, 2))
    exx = minus(vx, 0)
    eyy = minus(vy, 1)
    ezz = minus(vz, 2)
    div = exx + eyy + ezz
    sxx = sxx + COURANT * (lam * div + 2.0 * shear * exx)
    syy = syy + COURANT * (lam * div + 2.0 * shear * eyy)
    szz = szz + COURANT * (lam * div + 2.0 * shear * ezz)
    sxy = sxy + COURANT * shear * (plus(vy, 0) + plus(vx, 1))
    sxz = sxz + COURANT * shear * (plus(vz, 0) + plus(vx, 2))
    syz = syz + COURANT * shear * (plus(vz, 1) + plus(vy, 2))
    return [vx, vy, vz, sxx, syy, szz, sxy, sxz, syz]


def smooth(grad):
    padded = jnp.pad(grad, ((0, 0), (1, 1), (1, 1), (1, 1)))
    near = padded[:, 2:, 1:-1, 1:-1] + padded[:, :-2, 1:-1, 1:-1]
    near = near + padded[:, 1:-1, 2:, 1:-1] + padded[:, 1:-1, :-2, 1:-1]
    near = near + padded[:, 1:-1, 1:-1, 2:] + padded[:, 1:-1, 1:-1, :-2]
    return grad + KAPPA * (near - 6.0 * grad)


def reference(adjoint_state, forward_velocity, vp, shear_ratio, density, residuals, owner, cell):
    buoy = 1.0 / density
    speed_s = shear_ratio * vp
    shear = density * speed_s * speed_s
    lam = density * vp * vp - 2.0 * shear
    flat_cell = owner[:, 0] * (CX * NY * NZ) + cell
    finals = []
    glam = jnp.zeros(vp.shape, jnp.float32)
    gmu = jnp.zeros(vp.shape, jnp.float32)
    grho = jnp.zeros(vp.shape, jnp.float32)
    for group in range(SHOTS):
        fields = [adjoint_state[group, k] for k in range(9)]
        for step in range(STEPS):
            fields = advance(fields, buoy, lam, shear)
            szz_flat = fields[5].reshape(-1).at[flat_cell].add(residuals[group, step])
            fields[5] = szz_flat.reshape(vp.shape)
            ux, uy, uz = forward_velocity[group, step, 0], forward_velocity[group, step, 1], forward_velocity[group, step, 2]
            wx, wy, wz = forward_velocity[group, step + 1, 0], forward_velocity[group, step + 1, 1], forward_velocity[group, step + 1, 2]
            vx, vy, vz, sxx, syy, szz, sxy, sxz, syz = fields
            fxx = minus(ux, 0)
            fyy = minus(uy, 1)
            fzz = minus(uz, 2)
            glam = glam + (fxx + fyy + fzz) * (sxx + syy + szz)
            gmu = gmu + 2.0 * (fxx * sxx + fyy * syy + fzz * szz) + (plus(uy, 0) + plus(ux, 1)) * sxy + (plus(uz, 0) + plus(ux, 2)) * sxz + (plus(uz, 1) + plus(uy, 2)) * syz
            grho = grho + vx * (wx - ux) + vy * (wy - uy) + vz * (wz - uz)
        finals.append(jnp.stack(fields))
    grad = jnp.stack([glam, gmu, grho])
    for sweep in range(SWEEPS):
        grad = smooth(grad)
    return jnp.stack(finals), grad
```

```python
import functools

import jax
import jax.numpy as jnp
from jax import lax
from jax.experimental import pallas as pl
from jax.experimental.pallas import tpu as pltpu
from jax.sharding import PartitionSpec as P

STEPS = 3
CX, NY, NZ = 16, 64, 128
NX = 512
N_SPACE = 32
CH_DEV = 1024
CAP = 128
COURANT = 0.3
KAPPA = 0.15
ROWS = 32
PAD = 8
PY = NY + 2 * PAD
VX, VY, VZ, SXX, SYY, SZZ, SXY, SXZ, SYZ = range(9)
CHUNKS = (0, 3, 1, 2)
F32, BF16, I32 = jnp.float32, jnp.bfloat16, jnp.int32


def nt(a, b):
    return lax.dot_general(a, b, (((1,), (1,)), ((), ())), preferred_element_type=F32)


def lane_of(rows):
    return lax.broadcasted_iota(I32, (rows, NZ), 1)


def zminus(f):
    rolled = pltpu.roll(f, 1, 1)
    return f - jnp.where(lane_of(f.shape[0]) == 0, 0.0, rolled)


def zplus(f):
    rolled = pltpu.roll(f, NZ - 1, 1)
    return jnp.where(lane_of(f.shape[0]) == NZ - 1, 0.0, rolled) - f


def kernel(
    adj, fwd, vp_h, sr_h, dn_h, res, own, cell,
    out_adj, out_grad,
    f0, f1, f2, f3, f4, f5, f6, f7, f8,
    fw, dense, cb, cl, cm, g0, g1, g2,
    packed, arrived, a_one, b_one,
    gs, rb1, s2, rb2, h0, h1, og,
    load_f, load_w, load_p, out_sem,
    halo_s, halo_r, fh_s, fh_r, a2a_s, a2a_r,
    r1_s, r1_r, r2_s, r2_r, gx_s, gx_r,
):
    F = (f0, f1, f2, f3, f4, f5, f6, f7, f8)
    G = (g0, g1, g2)
    me = lax.axis_index("space")
    sh = lax.axis_index("shot")
    core = sh % 2
    chip = sh // 2
    has_left = me > 0
    has_right = me < N_SPACE - 1
    left = (me + N_SPACE - 1) % N_SPACE
    right = (me + 1) % N_SPACE
    mate = 2 * chip + (1 - core)
    cross = 2 * (1 - chip) + core
    inner = pl.ds(PAD, NY)

    loads_p = [pltpu.make_async_copy(src, dst, load_p.at[i]) for i, (src, dst) in enumerate(((vp_h, cl), (sr_h, cm), (dn_h, cb)))]
    loads_f = [pltpu.make_async_copy(adj.at[0, k], F[k].at[pl.ds(1, CX), inner], load_f.at[k]) for k in range(9)]
    loads_w = [pltpu.make_async_copy(fwd.at[0, t], fw.at[t, :, pl.ds(1, CX), inner], load_w.at[t]) for t in range(STEPS + 1)]
    for c in loads_p:
        c.start()
    for k in (SXX, SXY, SXZ, SYY, SYZ, SZZ, VX, VY, VZ):
        loads_f[k].start()
    for c in loads_w:
        c.start()

    zpad = jnp.zeros((PAD, NZ), F32)

    def zero_pads(x, carry):
        for k in (VX, VY, VZ, SYY, SXY, SYZ):
            F[k][x, pl.ds(0, PAD), :] = zpad
            F[k][x, pl.ds(PAD + NY, PAD), :] = zpad
        for t in range(STEPS):
            for k in range(3):
                fw[t, k, x, pl.ds(0, PAD), :] = zpad
                fw[t, k, x, pl.ds(PAD + NY, PAD), :] = zpad
        return carry

    lax.fori_loop(1, CX + 1, zero_pads, 0)

    def zero_h(x, carry):
        for k in range(3):
            h0[k, x, :, :] = jnp.zeros((40, NZ), F32)
        return carry

    lax.fori_loop(0, CX + 4, zero_h, 0)

    def zero_gs(i, carry):
        for k in range(3):
            for xx in range(2):
                gs[0, k, i, pl.ds(20 * xx, 2), :] = jnp.zeros((2, NZ), F32)
                gs[3, k, i, pl.ds(20 * xx + 18, 2), :] = jnp.zeros((2, NZ), F32)
        return carry

    lax.fori_loop(0, CX // 2, zero_gs, 0)
    zplane = jnp.zeros((NY, NZ), F32)

    @pl.when(me == 0)
    def _():
        for k in (VX, SXY, SXZ):
            F[k][0, inner, :] = zplane
        for t in range(STEPS):
            fw[t, 0, 0, inner, :] = zplane

    @pl.when(me == N_SPACE - 1)
    def _():
        for k in (SXX, VY, VZ):
            F[k][CX + 1, inner, :] = zplane
        for t in range(STEPS):
            for k in (1, 2):
                fw[t, k, CX + 1, inner, :] = zplane

    barrier = pltpu.get_barrier_semaphore()

    def greet(k, carry):
        pl.semaphore_signal(barrier, inc=1, device_id={"space": (me + k) % N_SPACE}, device_id_type=pl.DeviceIdType.MESH)
        return carry

    lax.fori_loop(1, N_SPACE, greet, 0)
    for other in (mate, cross):
        pl.semaphore_signal(barrier, inc=1, device_id={"shot": other}, device_id_type=pl.DeviceIdType.MESH)

    blk = 256
    upper = (lax.broadcasted_iota(I32, (blk, blk), 0) < lax.broadcasted_iota(I32, (blk, blk), 1)).astype(F32).astype(BF16)
    carry_n = jnp.zeros((N_SPACE, 1), F32)
    acc = jnp.zeros((N_SPACE * 16, CAP), F32)
    for b in range(CH_DEV // blk):
        lanes = pl.ds(b * blk, blk)
        o = own[:, lanes]
        oh = (o == lax.broadcasted_iota(I32, (N_SPACE, blk), 0)).astype(F32)
        ranks = jnp.dot(oh.astype(BF16), upper, preferred_element_type=F32) + carry_n
        carry_n = carry_n + jnp.sum(oh, axis=1, keepdims=True)
        rank = jnp.sum(oh * ranks, axis=0, keepdims=True)
        slot = (rank.astype(I32) == lax.broadcasted_iota(I32, (CAP, blk), 0)).astype(F32).astype(BF16)
        cl_ = cell[:, lanes]
        r = [res[t, :, lanes] for t in range(STEPS)]
        hi = [v.astype(BF16).astype(F32) for v in r]
        zero = jnp.zeros((1, blk), F32)
        rows = (
            hi
            + [(cl_ >> 13).astype(F32), ((cl_ >> 7) & 63).astype(F32), (cl_ & 127).astype(F32), zero, zero]
            + [a - h for a, h in zip(r, hi)]
            + [zero] * 5
        )
        payload = jnp.concatenate(rows, axis=0)
        lhs = (oh[:, None, :] * payload[None, :, :]).reshape(N_SPACE * 16, blk).astype(BF16)
        acc = acc + nt(lhs, slot)
    acc = acc.reshape(N_SPACE, 16, CAP)
    packed[...] = acc[:, :8, :] + acc[:, 8:, :]

    pl.semaphore_wait(barrier, N_SPACE + 1)

    def send(src, dst, s, r, to):
        return pltpu.make_async_remote_copy(
            src_ref=src, dst_ref=dst, send_sem=s, recv_sem=r, device_id={"space": to}, device_id_type=pl.DeviceIdType.MESH
        )

    def tail_to_right(step, j, k, src=None):
        src = F[k].at[CX, inner] if src is None else src
        return send(src, F[k].at[0, inner], halo_s.at[step, j], halo_r.at[step, j], right)

    def head_to_left(step, j, k, src=None):
        src = F[k].at[1, inner] if src is None else src
        return send(src, F[k].at[CX + 1, inner], halo_s.at[step, j], halo_r.at[step, j], left)

    def stress_halo(step):
        hb = step == 0
        to_left = [head_to_left(step, 0, SXX, adj.at[0, SXX, 0] if hb else None)]
        to_right = [
            tail_to_right(step, 1, SXY, adj.at[0, SXY, CX - 1] if hb else None),
            tail_to_right(step, 2, SXZ, adj.at[0, SXZ, CX - 1] if hb else None),
        ]
        return to_left, to_right

    def speed_halo(step):
        return [head_to_left(step, 3, VY), head_to_left(step, 4, VZ)], [tail_to_right(step, 5, VX)]

    def forward_halo():
        return (
            [send(fwd.at[0, pl.ds(0, STEPS), pl.ds(1, 2), 0], fw.at[pl.ds(0, STEPS), pl.ds(1, 2), CX + 1, inner], fh_s.at[0], fh_r.at[0], left)],
            [send(fwd.at[0, pl.ds(0, STEPS), 0, CX - 1], fw.at[pl.ds(0, STEPS), 0, 0, inner], fh_s.at[1], fh_r.at[1], right)],
        )

    def start(pair):
        @pl.when(has_left)
        def _():
            for c in pair[0]:
                c.start()

        @pl.when(has_right)
        def _():
            for c in pair[1]:
                c.start()

    def wait_recv(pair):
        @pl.when(has_right)
        def _():
            for c in pair[0]:
                c.wait_recv()

        @pl.when(has_left)
        def _():
            for c in pair[1]:
                c.wait_recv()

    def wait_send(pair):
        @pl.when(has_left)
        def _():
            for c in pair[0]:
                c.wait_send()

        @pl.when(has_right)
        def _():
            for c in pair[1]:
                c.wait_send()

    start(stress_halo(0))

    def channel_copy(k):
        to = (me + k) % N_SPACE
        return send(packed.at[to], arrived.at[me], a2a_s.at[k], a2a_r.at[k], to)

    def channel_start(k, carry):
        channel_copy(k).start()
        return carry

    lax.fori_loop(1, N_SPACE, channel_start, 0)
    start(forward_halo())
    arrived[me] = packed[me]

    for c in loads_p:
        c.wait()

    def params(x, carry):
        rho, vp, ratio = cb[x], cl[x], cm[x]
        vs = ratio * vp
        mu = rho * vs * vs
        cb[x] = COURANT * (1.0 / rho)
        cl[x] = COURANT * (rho * vp * vp - 2.0 * mu)
        cm[x] = COURANT * mu
        return carry

    lax.fori_loop(0, CX, params, 0)
    for c in loads_f:
        c.wait()

    def speeds(x, carry=0):
        for y in range(0, NY, ROWS):
            def at(k, dx=0, dy=0):
                return F[k][x + dx, pl.ds(PAD + y + dy, ROWS), :]

            here = pl.ds(PAD + y, ROWS)
            b = cb[x - 1, pl.ds(y, ROWS), :]
            sxy, sxz, syz = at(SXY), at(SXZ), at(SYZ)
            vx = at(VX) + b * ((at(SXX, 1) - at(SXX)) + (sxy - at(SXY, 0, -1)) + zminus(sxz))
            vy = at(VY) + b * ((sxy - at(SXY, -1)) + (at(SYY, 0, 1) - at(SYY)) + zminus(syz))
            vz = at(VZ) + b * ((sxz - at(SXZ, -1)) + (syz - at(SYZ, 0, -1)) + zplus(at(SZZ)))
            F[VX][x, here, :] = vx
            F[VY][x, here, :] = vy
            F[VZ][x, here, :] = vz
        return carry

    def stresses(step, x, carry=0):
        for y in range(0, NY, ROWS):
            def at(k, dx=0, dy=0):
                return F[k][x + dx, pl.ds(PAD + y + dy, ROWS), :]

            here = pl.ds(PAD + y, ROWS)
            flat = pl.ds(y, ROWS)
            lam, mu = cl[x - 1, flat, :], cm[x - 1, flat, :]
            vx, vy, vz = at(VX), at(VY), at(VZ)
            exx = vx - at(VX, -1)
            eyy = vy - at(VY, 0, -1)
            ezz = zminus(vz)
            base = lam * (exx + eyy + ezz)
            mu2 = mu + mu
            F[SXX][x, here, :] = at(SXX) + (base + mu2 * exx)
            F[SYY][x, here, :] = at(SYY) + (base + mu2 * eyy)
            F[SZZ][x, here, :] = at(SZZ) + (base + mu2 * ezz)
            F[SXY][x, here, :] = at(SXY) + mu * ((at(VY, 1) - vy) + (at(VX, 0, 1) - vx))
            F[SXZ][x, here, :] = at(SXZ) + mu * ((at(VZ, 1) - vz) + zplus(vx))
            F[SYZ][x, here, :] = at(SYZ) + mu * ((at(VZ, 0, 1) - vz) + zplus(vy))
        return carry

    def gradients(step, x, carry=0):
        for y in range(0, NY, ROWS):
            def at(k):
                return F[k][x, pl.ds(PAD + y, ROWS), :]

            def u(k, dx=0, dy=0):
                return fw[step, k, x + dx, pl.ds(PAD + y + dy, ROWS), :]

            def w(k):
                return fw[step + 1, k, x, pl.ds(PAD + y, ROWS), :]

            here = pl.ds(PAD + y, ROWS)
            flat = pl.ds(y, ROWS)
            sxx, syy = at(SXX), at(SYY)
            szz = at(SZZ) + dense[step, x - 1, flat, :]
            F[SZZ][x, here, :] = szz
            ux, uy, uz = u(0), u(1), u(2)
            fxx = ux - u(0, -1)
            fyy = uy - u(1, 0, -1)
            fzz = zminus(uz)
            lam = (fxx + fyy + fzz) * (sxx + syy + szz)
            mu = (
                2.0 * (fxx * sxx + fyy * syy + fzz * szz)
                + ((u(1, 1) - uy) + (u(0, 0, 1) - ux)) * at(SXY)
                + ((u(2, 1) - uz) + zplus(ux)) * at(SXZ)
                + ((u(2, 0, 1) - uz) + zplus(uy)) * at(SYZ)
            )
            rho = at(VX) * (w(0) - ux) + at(VY) * (w(1) - uy) + at(VZ) * (w(2) - uz)
            for ref, term in zip(G, (lam, mu, rho)):
                ref[x - 1, flat, :] = term if step == 0 else ref[x - 1, flat, :] + term
        return carry

    def densify():
        def channel_wait(k, carry):
            channel_copy(k).wait_recv()
            return carry

        lax.fori_loop(1, N_SPACE, channel_wait, 0)

        def one_hot(s, carry):
            lanes = pl.ds(pl.multiple_of(s * CAP, CAP), CAP)
            row = arrived[s]
            x, y, z = row[3:4].astype(I32), row[4:5].astype(I32), row[5:6].astype(I32)
            yone = (y == lax.broadcasted_iota(I32, (NY, CAP), 0)).astype(F32)
            zone = (z == lax.broadcasted_iota(I32, (NZ, CAP), 0)).astype(F32)
            for i in range(CX):
                a_one[pl.ds(i * NY, NY), lanes] = jnp.where(x == i, yone, 0.0).astype(BF16)
            for t in range(STEPS):
                v = row[t : t + 1]
                hi = v.astype(BF16).astype(F32)
                b_one[pl.ds(2 * t * NZ, NZ), lanes] = (zone * hi).astype(BF16)
                b_one[pl.ds((2 * t + 1) * NZ, NZ), lanes] = (zone * (v - hi)).astype(BF16)
            return carry

        lax.fori_loop(0, N_SPACE, one_hot, 0)

        def product(m, carry):
            got = nt(a_one[pl.ds(pl.multiple_of(m * 256, 256), 256), :], b_one[...])
            for t in range(STEPS):
                both = got[:, 2 * t * NZ : (2 * t + 1) * NZ] + got[:, (2 * t + 1) * NZ : (2 * t + 2) * NZ]
                dense[t, pl.ds(4 * m, 4), :, :] = both.reshape(4, NY, NZ)
            return carry

        lax.fori_loop(0, 4, product, 0)

    for step in range(STEPS):
        if step > 0:
            wait_send(speed_halo(step - 1))
        lax.fori_loop(2, CX, speeds, 0)
        wait_recv(stress_halo(step))
        speeds(1)
        speeds(CX)
        start(speed_halo(step))
        wait_send(stress_halo(step))
        lax.fori_loop(2, CX, functools.partial(stresses, step), 0)
        wait_recv(speed_halo(step))
        stresses(step, 1)
        stresses(step, CX)
        if step + 1 < STEPS:
            start(stress_halo(step + 1))
        if step == 0:
            densify()
            for c in loads_w:
                c.wait()
            wait_recv(forward_halo())
        lax.fori_loop(1, CX + 1, functools.partial(gradients, step), 0)
    wait_send(speed_halo(STEPS - 1))
    wait_send(forward_halo())

    def channel_sent(k, carry):
        channel_copy(k).wait_send()
        return carry

    lax.fori_loop(1, N_SPACE, channel_sent, 0)
    stores = [pltpu.make_async_copy(F[k].at[pl.ds(1, CX), inner], out_adj.at[0, k], out_sem.at[k]) for k in range(9)]
    for c in stores:
        c.start()

    def to_mate(ch):
        return [
            pltpu.make_async_remote_copy(
                src_ref=gs.at[2 * j + 1 - core, :, pl.ds(2 * ch, 2)],
                dst_ref=rb1.at[j, :, pl.ds(2 * ch, 2)],
                send_sem=r1_s.at[ch, j],
                recv_sem=r1_r.at[ch, j],
                device_id={"shot": mate},
                device_id_type=pl.DeviceIdType.MESH,
            )
            for j in range(2)
        ]

    def to_cross(ch):
        return pltpu.make_async_remote_copy(
            src_ref=s2.at[:, pl.ds(2 * ch, 2)],
            dst_ref=rb2.at[:, pl.ds(2 * ch, 2)],
            send_sem=r2_s.at[ch],
            recv_sem=r2_r.at[ch],
            device_id={"shot": cross},
            device_id_type=pl.DeviceIdType.MESH,
        )

    def slabs(i, carry):
        for k in range(3):
            for xx in range(2):
                for s in range(4):
                    lo, hi = max(0, 16 * s - 2), min(NY, 16 * s + 18)
                    off = 20 * xx + lo - (16 * s - 2)
                    gs[s, k, i, pl.ds(off, hi - lo), :] = G[k][2 * i + xx, pl.ds(lo, hi - lo), :]
        return carry

    for ch in CHUNKS:
        lax.fori_loop(2 * ch, 2 * ch + 2, slabs, 0)
        for c in to_mate(ch):
            c.start()

    def sum_cross(i, carry):
        for k in range(3):
            s2[k, i] = gs[2 * (1 - chip) + core, k, i] + rb1[1 - chip, k, i]
        return carry

    for ch in CHUNKS:
        for c in to_mate(ch):
            c.wait_recv()
        lax.fori_loop(2 * ch, 2 * ch + 2, sum_cross, 0)
        to_cross(ch).start()

    def sum_own(i, carry):
        for k in range(3):
            for xx in range(2):
                part = pl.ds(20 * xx, 20)
                total = (gs[2 * chip + core, k, i, part, :] + rb1[chip, k, i, part, :]) + rb2[k, i, part, :]
                h0[k, 2 + 2 * i + xx, pl.ds(8, 20), :] = total
        return carry

    rim = pl.ds(8, 24)
    grad_halo = (
        [send(h0.at[:, pl.ds(2, 2), rim], h0.at[:, pl.ds(CX + 2, 2), rim], gx_s.at[0], gx_r.at[0], left)],
        [send(h0.at[:, pl.ds(CX, 2), rim], h0.at[:, pl.ds(0, 2), rim], gx_s.at[1], gx_r.at[1], right)],
    )
    for n, ch in enumerate(CHUNKS):
        to_cross(ch).wait_recv()
        lax.fori_loop(2 * ch, 2 * ch + 2, sum_own, 0)
        if n == 1:
            start(grad_halo)
    wait_recv(grad_halo)
    wait_send(grad_halo)

    def near(h, k, p, lo, n):
        def at(dp=0, dy=0):
            return h[k, p + dp, pl.ds(lo + dy, n), :]

        mid = at()
        lane = lane_of(n)
        total = at(1) + at(-1) + at(0, 1) + at(0, -1)
        total = total + jnp.where(lane == NZ - 1, 0.0, pltpu.roll(mid, NZ - 1, 1)) + jnp.where(lane == 0, 0.0, pltpu.roll(mid, 1, 1))
        return mid + KAPPA * (total - 6.0 * mid)

    def sweep_one(p, carry):
        gx = CX * me + p - 2
        gy = 16 * sh - 2 + lax.broadcasted_iota(I32, (24, NZ), 0)
        keep = (gy >= 0) & (gy < NY) & (gx >= 0) & (gx < NX)
        for k in range(3):
            h1[k, p, rim, :] = jnp.where(keep, near(h0, k, p, 8, 24), 0.0)
        return carry

    lax.fori_loop(1, CX + 3, sweep_one, 0)

    def sweep_two(x, carry):
        for k in range(3):
            og[k, x] = near(h1, k, x + 2, 10, 16)
        return carry

    lax.fori_loop(0, CX, sweep_two, 0)
    grad_out = pltpu.make_async_copy(og, out_grad, out_sem.at[9])
    grad_out.start()
    for ch in CHUNKS:
        for c in to_mate(ch):
            c.wait_send()
        to_cross(ch).wait_send()
    for c in stores:
        c.wait()
    grad_out.wait()


def local(adjoint_state, forward_velocity, vp, shear_ratio, density, residuals, owner, cell):
    res = residuals.reshape(STEPS, 1, CH_DEV)
    own = owner.reshape(1, CH_DEV)
    cells = cell.reshape(1, CH_DEV)
    hbm = pl.BlockSpec(memory_space=pl.ANY)
    vmem = pl.BlockSpec(memory_space=pltpu.VMEM)
    volume = pltpu.VMEM((CX, NY, NZ), F32)
    dma = pltpu.SemaphoreType.DMA
    scratch = (
        [pltpu.VMEM((CX + 2, PY, NZ), F32)] * 9
        + [
            pltpu.VMEM((STEPS + 1, 3, CX + 2, PY, NZ), F32),
            pltpu.VMEM((STEPS, CX, NY, NZ), F32),
        ]
        + [volume] * 6
        + [
            pltpu.VMEM((N_SPACE, 8, CAP), F32),
            pltpu.VMEM((N_SPACE, 8, CAP), F32),
            pltpu.VMEM((CX * NY, N_SPACE * CAP), BF16),
            pltpu.VMEM((2 * STEPS * NZ, N_SPACE * CAP), BF16),
            pltpu.VMEM((4, 3, CX // 2, 40, NZ), F32),
            pltpu.VMEM((2, 3, CX // 2, 40, NZ), F32),
            pltpu.VMEM((3, CX // 2, 40, NZ), F32),
            pltpu.VMEM((3, CX // 2, 40, NZ), F32),
            pltpu.VMEM((3, CX + 4, 40, NZ), F32),
            pltpu.VMEM((3, CX + 4, 40, NZ), F32),
            pltpu.VMEM((3, CX, 16, NZ), F32),
        ]
        + [dma((9,)), dma((4,)), dma((3,)), dma((10,))]
        + [dma((STEPS, 6)), dma((STEPS, 6)), dma((2,)), dma((2,)), dma((N_SPACE,)), dma((N_SPACE,))]
        + [dma((4, 2)), dma((4, 2)), dma((4,)), dma((4,)), dma((2,)), dma((2,))]
    )
    return pl.pallas_call(
        kernel,
        out_shape=(
            jax.ShapeDtypeStruct((1, 9, CX, NY, NZ), F32),
            jax.ShapeDtypeStruct((3, CX, 16, NZ), F32),
        ),
        in_specs=[hbm] * 5 + [vmem] * 3,
        out_specs=(hbm, hbm),
        scratch_shapes=scratch,
        compiler_params=pltpu.CompilerParams(collective_id=0, has_side_effects=True, vmem_limit_bytes=60 * 1024 * 1024),
    )(adjoint_state, forward_velocity, vp, shear_ratio, density, res, own, cells)


def solution(mesh):
    in_specs = (
        P("shot", None, "space", None, None),
        P("shot", None, None, "space", None, None),
        P("space", None, None),
        P("space", None, None),
        P("space", None, None),
        P("shot", None, "space"),
        P("space", None),
        P("space"),
    )
    out_specs = (P("shot", None, "space", None, None), P(None, "space", "shot", None))
    return jax.shard_map(local, mesh=mesh, in_specs=in_specs, out_specs=out_specs, check_vma=False)
```

```python
import functools

import jax
import jax.numpy as jnp
from jax import lax
from jax.experimental import pallas as pl
from jax.experimental.pallas import tpu as pltpu
from jax.sharding import PartitionSpec as P

STEPS = 3
CX, NY, NZ = 16, 64, 128
NX = 512
N_SPACE = 32
CH_DEV = 1024
CAP = 128
COURANT = 0.3
KAPPA = 0.15
ROWS = 32
PAD = 8
PY = NY + 2 * PAD
VX, VY, VZ, SXX, SYY, SZZ, SXY, SXZ, SYZ = range(9)
GROUPS = ((0, 1), (7, 1), (1, 2), (5, 2), (3, 2))
F32, BF16, I32 = jnp.float32, jnp.bfloat16, jnp.int32


def nt(a, b):
    return lax.dot_general(a, b, (((1,), (1,)), ((), ())), preferred_element_type=F32)


def lane_of(rows):
    return lax.broadcasted_iota(I32, (rows, NZ), 1)


def zminus(f):
    rolled = pltpu.roll(f, 1, 1)
    return f - jnp.where(lane_of(f.shape[0]) == 0, 0.0, rolled)


def zplus(f):
    rolled = pltpu.roll(f, NZ - 1, 1)
    return jnp.where(lane_of(f.shape[0]) == NZ - 1, 0.0, rolled) - f


def kernel(
    adj, fwd, vp_h, sr_h, dn_h, res_h, own_h, cell_h,
    f0, f1, f2, f3, f4, f5, f6, f7, f8, h0,
    fw, dense, cb, cl, cm, g0, g1, g2,
    to_left, to_right, from_left, from_right, edge_b, rho_end,
    res, own, cell, packed, arrived, a_one, b_one,
    gs, rb1, s2, rb2,
    load_f, load_w, load_p, load_e, load_c,
    halo_s, halo_r, eb_s, eb_r, fh_s, fh_r, a2a_s, a2a_r,
    r1_s, r1_r, r2_s, r2_r, gx_s, gx_r,
):
    F = (f0, f1, f2, f3, f4, f5, f6, f7, f8)
    G = (g0, g1, g2)
    me = lax.axis_index("space")
    sh = lax.axis_index("shot")
    core = sh % 2
    chip = sh // 2
    has_left = me > 0
    has_right = me < N_SPACE - 1
    left = (me + N_SPACE - 1) % N_SPACE
    right = (me + 1) % N_SPACE
    mate = 2 * chip + (1 - core)
    cross = 2 * (1 - chip) + core
    inner = pl.ds(PAD, NY)

    ends = ((0, 0), (1, CX - 1))
    middle = pl.ds(1, CX - 2)
    loads_e = [pltpu.make_async_copy(dn_h.at[x], cb.at[x], load_e.at[9, i]) for i, x in ends]
    loads_e += [pltpu.make_async_copy(adj.at[0, k, x], F[k].at[x + 1, inner], load_e.at[k, i]) for k in range(9) for i, x in ends]
    loads_p = [pltpu.make_async_copy(vp_h, cl, load_p.at[0]), pltpu.make_async_copy(sr_h, cm, load_p.at[1])]
    loads_p.append(pltpu.make_async_copy(dn_h.at[middle], cb.at[middle], load_p.at[2]))
    loads_f = [pltpu.make_async_copy(adj.at[0, k, middle], F[k].at[pl.ds(2, CX - 2), inner], load_f.at[k]) for k in range(9)]
    loads_w = [pltpu.make_async_copy(fwd.at[0, t], fw.at[t, :, pl.ds(1, CX), inner], load_w.at[t]) for t in range(STEPS + 1)]
    loads_c = [pltpu.make_async_copy(src, dst, load_c.at[i]) for i, (src, dst) in enumerate(((own_h, own), (cell_h, cell), (res_h, res)))]
    for c in loads_c + loads_e + loads_p + loads_f + loads_w:
        c.start()

    zpad = jnp.zeros((PAD, NZ), F32)

    def zero_pads(x, carry):
        for k in (VX, VY, VZ, SYY, SXY, SYZ):
            F[k][x, pl.ds(0, PAD), :] = zpad
            F[k][x, pl.ds(PAD + NY, PAD), :] = zpad
        for t in range(STEPS):
            for k in range(3):
                fw[t, k, x, pl.ds(0, PAD), :] = zpad
                fw[t, k, x, pl.ds(PAD + NY, PAD), :] = zpad
        return carry

    lax.fori_loop(1, CX + 1, zero_pads, 0)

    def zero_h(x, carry):
        for k in range(3):
            h0[k, x, :, :] = jnp.zeros((40, NZ), F32)
        return carry

    lax.fori_loop(0, CX + 4, zero_h, 0)

    def zero_gs(i, carry):
        for k in range(3):
            for xx in range(2):
                gs[0, k, i, pl.ds(20 * xx, 2), :] = jnp.zeros((2, NZ), F32)
                gs[3, k, i, pl.ds(20 * xx + 18, 2), :] = jnp.zeros((2, NZ), F32)
        return carry

    lax.fori_loop(0, CX // 2, zero_gs, 0)
    zplane = jnp.zeros((NY, NZ), F32)

    @pl.when(me == 0)
    def _():
        edge_b[0] = zplane
        for t in range(STEPS):
            fw[t, 0, 0, inner, :] = zplane
            for k in range(3):
                from_left[t, k] = zplane

    @pl.when(me == N_SPACE - 1)
    def _():
        edge_b[1] = zplane
        for t in range(STEPS):
            for k in range(3):
                from_right[t, k] = zplane
            for k in (1, 2):
                fw[t, k, CX + 1, inner, :] = zplane

    barrier = pltpu.get_barrier_semaphore()

    def greet(k, carry):
        pl.semaphore_signal(barrier, inc=1, device_id={"space": (me + k) % N_SPACE}, device_id_type=pl.DeviceIdType.MESH)
        return carry

    lax.fori_loop(1, N_SPACE, greet, 0)
    for other in (mate, cross):
        pl.semaphore_signal(barrier, inc=1, device_id={"shot": other}, device_id_type=pl.DeviceIdType.MESH)

    def edges_out(step):
        for y in range(0, NY, ROWS):
            def at(k, x, dy=0):
                return F[k][x, pl.ds(PAD + y + dy, ROWS), :]

            rows = pl.ds(y, ROWS)
            b = cb[0, rows, :]
            syz = at(SYZ, 1)
            to_left[step, 0, rows, :] = at(SXX, 1)
            to_left[step, 1, rows, :] = at(VY, 1) + b * (at(SXY, 1) + (at(SYY, 1, 1) - at(SYY, 1)) + zminus(syz))
            to_left[step, 2, rows, :] = at(VZ, 1) + b * (at(SXZ, 1) + (syz - at(SYZ, 1, -1)) + zplus(at(SZZ, 1)))
            b = cb[CX - 1, rows, :]
            sxy, sxz = at(SXY, CX), at(SXZ, CX)
            to_right[step, 0, rows, :] = at(VX, CX) + b * ((sxy - at(SXY, CX, -1)) + zminus(sxz) - at(SXX, CX))
            to_right[step, 1, rows, :] = sxy
            to_right[step, 2, rows, :] = sxz

    def edges_in(step):
        for y in range(0, NY, ROWS):
            rows = pl.ds(y, ROWS)
            here = pl.ds(PAD + y, ROWS)
            b = edge_b[0, rows, :]
            F[VX][0, here, :] = from_left[step, 0, rows, :] + b * F[SXX][1, here, :]
            F[SXY][0, here, :] = from_left[step, 1, rows, :]
            F[SXZ][0, here, :] = from_left[step, 2, rows, :]
            b = edge_b[1, rows, :]
            F[SXX][CX + 1, here, :] = from_right[step, 0, rows, :]
            F[VY][CX + 1, here, :] = from_right[step, 1, rows, :] - b * F[SXY][CX, here, :]
            F[VZ][CX + 1, here, :] = from_right[step, 2, rows, :] - b * F[SXZ][CX, here, :]

    for c in loads_e:
        c.wait()
    for i, x in ends:
        rho = cb[x]
        rho_end[i] = rho
        cb[x] = COURANT * (1.0 / rho)
    edges_out(0)

    for c in loads_c:
        c.wait()
    blk = 256
    upper = (lax.broadcasted_iota(I32, (blk, blk), 0) < lax.broadcasted_iota(I32, (blk, blk), 1)).astype(F32).astype(BF16)
    carry_n = jnp.zeros((N_SPACE, 1), F32)
    acc = jnp.zeros((N_SPACE * 16, CAP), F32)
    for b in range(CH_DEV // blk):
        lanes = pl.ds(b * blk, blk)
        o = own[:, lanes]
        oh = (o == lax.broadcasted_iota(I32, (N_SPACE, blk), 0)).astype(F32)
        ranks = jnp.dot(oh.astype(BF16), upper, preferred_element_type=F32) + carry_n
        carry_n = carry_n + jnp.sum(oh, axis=1, keepdims=True)
        rank = jnp.sum(oh * ranks, axis=0, keepdims=True)
        slot = (rank.astype(I32) == lax.broadcasted_iota(I32, (CAP, blk), 0)).astype(F32).astype(BF16)
        cl_ = cell[:, lanes]
        r = [res[t, :, lanes] for t in range(STEPS)]
        hi = [v.astype(BF16).astype(F32) for v in r]
        zero = jnp.zeros((1, blk), F32)
        rows = (
            hi
            + [(cl_ >> 13).astype(F32), ((cl_ >> 7) & 63).astype(F32), (cl_ & 127).astype(F32), zero, zero]
            + [a - h for a, h in zip(r, hi)]
            + [zero] * 5
        )
        payload = jnp.concatenate(rows, axis=0)
        lhs = (oh[:, None, :] * payload[None, :, :]).reshape(N_SPACE * 16, blk).astype(BF16)
        acc = acc + nt(lhs, slot)
    acc = acc.reshape(N_SPACE, 16, CAP)
    packed[...] = acc[:, :8, :] + acc[:, 8:, :]

    pl.semaphore_wait(barrier, N_SPACE + 1)

    def send(src, dst, s, r, to):
        return pltpu.make_async_remote_copy(
            src_ref=src, dst_ref=dst, send_sem=s, recv_sem=r, device_id={"space": to}, device_id_type=pl.DeviceIdType.MESH
        )

    def edge_halo(step):
        return (
            [send(to_left.at[step], from_right.at[step], halo_s.at[step, 0], halo_r.at[step, 0], left)],
            [send(to_right.at[step], from_left.at[step], halo_s.at[step, 1], halo_r.at[step, 1], right)],
        )

    def density_halo():
        return (
            [send(dn_h.at[0], edge_b.at[1], eb_s.at[0], eb_r.at[0], left)],
            [send(dn_h.at[CX - 1], edge_b.at[0], eb_s.at[1], eb_r.at[1], right)],
        )

    def forward_halo():
        return (
            [send(fwd.at[0, pl.ds(0, STEPS), pl.ds(1, 2), 0], fw.at[pl.ds(0, STEPS), pl.ds(1, 2), CX + 1, inner], fh_s.at[0], fh_r.at[0], left)],
            [send(fwd.at[0, pl.ds(0, STEPS), 0, CX - 1], fw.at[pl.ds(0, STEPS), 0, 0, inner], fh_s.at[1], fh_r.at[1], right)],
        )

    def start(pair):
        @pl.when(has_left)
        def _():
            for c in pair[0]:
                c.start()

        @pl.when(has_right)
        def _():
            for c in pair[1]:
                c.start()

    def wait_recv(pair):
        @pl.when(has_right)
        def _():
            for c in pair[0]:
                c.wait_recv()

        @pl.when(has_left)
        def _():
            for c in pair[1]:
                c.wait_recv()

    def wait_send(pair):
        @pl.when(has_left)
        def _():
            for c in pair[0]:
                c.wait_send()

        @pl.when(has_right)
        def _():
            for c in pair[1]:
                c.wait_send()

    start(edge_halo(0))
    start(density_halo())

    def channel_copy(k):
        to = (me + k) % N_SPACE
        return send(packed.at[to], arrived.at[me], a2a_s.at[k], a2a_r.at[k], to)

    def channel_start(k, carry):
        channel_copy(k).start()
        return carry

    lax.fori_loop(1, N_SPACE, channel_start, 0)
    start(forward_halo())
    arrived[me] = packed[me]

    for c in loads_p:
        c.wait()

    def lame(x, rho):
        vp, ratio = cl[x], cm[x]
        vs = ratio * vp
        mu = rho * vs * vs
        cl[x] = COURANT * (rho * vp * vp - 2.0 * mu)
        cm[x] = COURANT * mu

    def params(x, carry):
        rho = cb[x]
        cb[x] = COURANT * (1.0 / rho)
        lame(x, rho)
        return carry

    lax.fori_loop(1, CX - 1, params, 0)
    for i, x in ends:
        lame(x, rho_end[i])
    for c in loads_f:
        c.wait()

    def speeds(x, carry=0):
        for y in range(0, NY, ROWS):
            def at(k, dx=0, dy=0):
                return F[k][x + dx, pl.ds(PAD + y + dy, ROWS), :]

            here = pl.ds(PAD + y, ROWS)
            b = cb[x - 1, pl.ds(y, ROWS), :]
            sxy, sxz, syz = at(SXY), at(SXZ), at(SYZ)
            vx = at(VX) + b * ((at(SXX, 1) - at(SXX)) + (sxy - at(SXY, 0, -1)) + zminus(sxz))
            vy = at(VY) + b * ((sxy - at(SXY, -1)) + (at(SYY, 0, 1) - at(SYY)) + zminus(syz))
            vz = at(VZ) + b * ((sxz - at(SXZ, -1)) + (syz - at(SYZ, 0, -1)) + zplus(at(SZZ)))
            F[VX][x, here, :] = vx
            F[VY][x, here, :] = vy
            F[VZ][x, here, :] = vz
        return carry

    def stresses(step, x, carry=0):
        inject = step > 0
        for y in range(0, NY, ROWS):
            def at(k, dx=0, dy=0):
                return F[k][x + dx, pl.ds(PAD + y + dy, ROWS), :]

            here = pl.ds(PAD + y, ROWS)
            flat = pl.ds(y, ROWS)
            lam, mu = cl[x - 1, flat, :], cm[x - 1, flat, :]
            vx, vy, vz = at(VX), at(VY), at(VZ)
            exx = vx - at(VX, -1)
            eyy = vy - at(VY, 0, -1)
            ezz = zminus(vz)
            base = lam * (exx + eyy + ezz)
            mu2 = mu + mu
            F[SXX][x, here, :] = at(SXX) + (base + mu2 * exx)
            F[SYY][x, here, :] = at(SYY) + (base + mu2 * eyy)
            szz = at(SZZ) + (base + mu2 * ezz)
            F[SZZ][x, here, :] = szz + dense[step, x - 1, flat, :] if inject else szz
            F[SXY][x, here, :] = at(SXY) + mu * ((at(VY, 1) - vy) + (at(VX, 0, 1) - vx))
            F[SXZ][x, here, :] = at(SXZ) + mu * ((at(VZ, 1) - vz) + zplus(vx))
            F[SYZ][x, here, :] = at(SYZ) + mu * ((at(VZ, 0, 1) - vz) + zplus(vy))
        return carry

    def gradients(step, x, carry=0):
        for y in range(0, NY, ROWS):
            def at(k):
                return F[k][x, pl.ds(PAD + y, ROWS), :]

            def u(k, dx=0, dy=0):
                return fw[step, k, x + dx, pl.ds(PAD + y + dy, ROWS), :]

            def w(k):
                return fw[step + 1, k, x, pl.ds(PAD + y, ROWS), :]

            flat = pl.ds(y, ROWS)
            sxx, syy, szz = at(SXX), at(SYY), at(SZZ)
            ux, uy, uz = u(0), u(1), u(2)
            fxx = ux - u(0, -1)
            fyy = uy - u(1, 0, -1)
            fzz = zminus(uz)
            lam = (fxx + fyy + fzz) * (sxx + syy + szz)
            mu = (
                2.0 * (fxx * sxx + fyy * syy + fzz * szz)
                + ((u(1, 1) - uy) + (u(0, 0, 1) - ux)) * at(SXY)
                + ((u(2, 1) - uz) + zplus(ux)) * at(SXZ)
                + ((u(2, 0, 1) - uz) + zplus(uy)) * at(SYZ)
            )
            rho = at(VX) * (w(0) - ux) + at(VY) * (w(1) - uy) + at(VZ) * (w(2) - uz)
            for ref, term in zip(G, (lam, mu, rho)):
                ref[x - 1, flat, :] = term if step == 0 else ref[x - 1, flat, :] + term
        return carry

    def densify():
        def channel_wait(k, carry):
            channel_copy(k).wait_recv()
            return carry

        lax.fori_loop(1, N_SPACE, channel_wait, 0)

        def one_hot(s, carry):
            lanes = pl.ds(pl.multiple_of(s * CAP, CAP), CAP)
            row = arrived[s]
            x, y, z = row[3:4].astype(I32), row[4:5].astype(I32), row[5:6].astype(I32)
            yone = (y == lax.broadcasted_iota(I32, (NY, CAP), 0)).astype(F32)
            zone = (z == lax.broadcasted_iota(I32, (NZ, CAP), 0)).astype(F32)
            for i in range(CX):
                a_one[pl.ds(i * NY, NY), lanes] = jnp.where(x == i, yone, 0.0).astype(BF16)
            for t in range(STEPS):
                v = row[t : t + 1]
                hi = v.astype(BF16).astype(F32)
                b_one[pl.ds(2 * t * NZ, NZ), lanes] = (zone * hi).astype(BF16)
                b_one[pl.ds((2 * t + 1) * NZ, NZ), lanes] = (zone * (v - hi)).astype(BF16)
            return carry

        lax.fori_loop(0, N_SPACE, one_hot, 0)

        def product(m, carry):
            got = nt(a_one[pl.ds(pl.multiple_of(m * 256, 256), 256), :], b_one[...])
            for t in range(STEPS):
                both = got[:, 2 * t * NZ : (2 * t + 1) * NZ] + got[:, (2 * t + 1) * NZ : (2 * t + 2) * NZ]
                dense[t, pl.ds(4 * m, 4), :, :] = both.reshape(4, NY, NZ)
            return carry

        lax.fori_loop(0, 4, product, 0)

        def inject(x, carry):
            F[SZZ][x, inner, :] = F[SZZ][x, inner, :] + dense[0, x - 1]
            return carry

        lax.fori_loop(1, CX + 1, inject, 0)

    for step in range(STEPS):
        lax.fori_loop(2, CX, speeds, 0)
        lax.fori_loop(3, CX - 1, functools.partial(stresses, step), 0)
        wait_recv(edge_halo(step))
        if step == 0:
            wait_recv(density_halo())
            for i in range(2):
                @pl.when(has_left if i == 0 else has_right)
                def _():
                    edge_b[i] = COURANT * (1.0 / edge_b[i])
        edges_in(step)
        speeds(1)
        speeds(CX)
        stresses(step, 1)
        stresses(step, CX)
        if step == 0:
            stresses(step, 2)
            stresses(step, CX - 1)
            densify()
        if step + 1 < STEPS:
            edges_out(step + 1)
            start(edge_halo(step + 1))
        if step > 0:
            stresses(step, 2)
            stresses(step, CX - 1)
        if step == 0:
            for c in loads_w:
                c.wait()
            wait_recv(forward_halo())
        if step + 1 < STEPS:
            lax.fori_loop(1, CX + 1, functools.partial(gradients, step), 0)

    def to_mate(n):
        pairs = pl.ds(*GROUPS[n])
        return [
            pltpu.make_async_remote_copy(
                src_ref=gs.at[2 * j + 1 - core, :, pairs],
                dst_ref=rb1.at[j, :, pairs],
                send_sem=r1_s.at[n, j],
                recv_sem=r1_r.at[n, j],
                device_id={"shot": mate},
                device_id_type=pl.DeviceIdType.MESH,
            )
            for j in range(2)
        ]

    def to_cross(n):
        pairs = pl.ds(*GROUPS[n])
        return pltpu.make_async_remote_copy(
            src_ref=s2.at[:, pairs],
            dst_ref=rb2.at[:, pairs],
            send_sem=r2_s.at[n],
            recv_sem=r2_r.at[n],
            device_id={"shot": cross},
            device_id_type=pl.DeviceIdType.MESH,
        )

    def pairs_of(n, body):
        first, count = GROUPS[n]
        lax.fori_loop(first, first + count, body, 0)

    def slabs(i, carry):
        for k in range(3):
            for xx in range(2):
                for s in range(4):
                    lo, hi = max(0, 16 * s - 2), min(NY, 16 * s + 18)
                    off = 20 * xx + lo - (16 * s - 2)
                    gs[s, k, i, pl.ds(off, hi - lo), :] = G[k][2 * i + xx, pl.ds(lo, hi - lo), :]
        return carry

    def sum_cross(i, carry):
        for k in range(3):
            s2[k, i] = gs[2 * (1 - chip) + core, k, i] + rb1[1 - chip, k, i]
        return carry

    def pass_on(n):
        for c in to_mate(n):
            c.wait_recv()
        pairs_of(n, sum_cross)
        to_cross(n).start()

    for n, (first, count) in enumerate(GROUPS):
        lax.fori_loop(2 * first + 1, 2 * (first + count) + 1, functools.partial(gradients, STEPS - 1), 0)
        pairs_of(n, slabs)
        for c in to_mate(n):
            c.start()
        if n > 0:
            pass_on(n - 1)
    pass_on(len(GROUPS) - 1)

    def sum_own(i, carry):
        for k in range(3):
            for xx in range(2):
                part = pl.ds(20 * xx, 20)
                total = (gs[2 * chip + core, k, i, part, :] + rb1[chip, k, i, part, :]) + rb2[k, i, part, :]
                h0[k, 2 + 2 * i + xx, pl.ds(8, 20), :] = total
        return carry

    rim = pl.ds(8, 24)
    grad_halo = (
        [send(h0.at[:, pl.ds(2, 2), rim], h0.at[:, pl.ds(CX + 2, 2), rim], gx_s.at[0], gx_r.at[0], left)],
        [send(h0.at[:, pl.ds(CX, 2), rim], h0.at[:, pl.ds(0, 2), rim], gx_s.at[1], gx_r.at[1], right)],
    )
    for n in range(len(GROUPS)):
        to_cross(n).wait_recv()
        pairs_of(n, sum_own)
        if n == 1:
            start(grad_halo)
    wait_recv(grad_halo)
    wait_send(grad_halo)

    for step in range(STEPS):
        wait_send(edge_halo(step))
    wait_send(density_halo())
    wait_send(forward_halo())

    def channel_sent(k, carry):
        channel_copy(k).wait_send()
        return carry

    lax.fori_loop(1, N_SPACE, channel_sent, 0)
    for n in range(len(GROUPS)):
        for c in to_mate(n):
            c.wait_send()
        to_cross(n).wait_send()


def finish(f0, f1, f2, f3, f4, f5, f6, f7, f8, h0, out_adj, out_grad, h1, og, sem):
    me = lax.axis_index("space")
    sh = lax.axis_index("shot")
    fields = (f0, f1, f2, f3, f4, f5, f6, f7, f8)
    stores = [pltpu.make_async_copy(f.at[pl.ds(1, CX), pl.ds(PAD, NY)], out_adj.at[0, k], sem.at[k]) for k, f in enumerate(fields)]
    for c in stores:
        c.start()

    def near(h, k, p, lo, n):
        def at(dp=0, dy=0):
            return h[k, p + dp, pl.ds(lo + dy, n), :]

        mid = at()
        lane = lane_of(n)
        total = at(1) + at(-1) + at(0, 1) + at(0, -1)
        total = total + jnp.where(lane == NZ - 1, 0.0, pltpu.roll(mid, NZ - 1, 1)) + jnp.where(lane == 0, 0.0, pltpu.roll(mid, 1, 1))
        return mid + KAPPA * (total - 6.0 * mid)

    def sweep_one(p, carry):
        gx = CX * me + p - 2
        gy = 16 * sh - 2 + lax.broadcasted_iota(I32, (24, NZ), 0)
        keep = (gy >= 0) & (gy < NY) & (gx >= 0) & (gx < NX)
        for k in range(3):
            h1[k, p, pl.ds(8, 24), :] = jnp.where(keep, near(h0, k, p, 8, 24), 0.0)
        return carry

    lax.fori_loop(1, CX + 3, sweep_one, 0)

    def sweep_two(x, carry):
        for k in range(3):
            og[k, x] = near(h1, k, x + 2, 10, 16)
        return carry

    lax.fori_loop(0, CX, sweep_two, 0)
    grad_out = pltpu.make_async_copy(og, out_grad, sem.at[9])
    grad_out.start()
    grad_out.wait()
    for c in stores:
        c.wait()


def local(adjoint_state, forward_velocity, vp, shear_ratio, density, residuals, owner, cell):
    res = residuals.reshape(STEPS, 1, CH_DEV)
    own = owner.reshape(1, CH_DEV)
    cells = cell.reshape(1, CH_DEV)
    hbm = pl.BlockSpec(memory_space=pltpu.HBM)
    vmem = pl.BlockSpec(memory_space=pltpu.VMEM)
    volume = pltpu.VMEM((CX, NY, NZ), F32)
    dma = pltpu.SemaphoreType.DMA
    edges = pltpu.VMEM((STEPS, 3, NY, NZ), F32)
    pair = pltpu.VMEM((2, NY, NZ), F32)
    count = len(GROUPS)
    scratch = (
        [
            pltpu.VMEM((STEPS + 1, 3, CX + 2, PY, NZ), F32),
            pltpu.VMEM((STEPS, CX, NY, NZ), F32),
        ]
        + [volume] * 6
        + [edges] * 4
        + [pair] * 2
        + [
            pltpu.VMEM((STEPS, 1, CH_DEV), F32),
            pltpu.VMEM((1, CH_DEV), I32),
            pltpu.VMEM((1, CH_DEV), I32),
            pltpu.VMEM((N_SPACE, 8, CAP), F32),
            pltpu.VMEM((N_SPACE, 8, CAP), F32),
            pltpu.VMEM((CX * NY, N_SPACE * CAP), BF16),
            pltpu.VMEM((2 * STEPS * NZ, N_SPACE * CAP), BF16),
            pltpu.VMEM((4, 3, CX // 2, 40, NZ), F32),
            pltpu.VMEM((2, 3, CX // 2, 40, NZ), F32),
            pltpu.VMEM((3, CX // 2, 40, NZ), F32),
            pltpu.VMEM((3, CX // 2, 40, NZ), F32),
        ]
        + [dma((9,)), dma((4,)), dma((3,)), dma((10, 2)), dma((3,))]
        + [dma((STEPS, 2)), dma((STEPS, 2)), dma((2,)), dma((2,)), dma((2,)), dma((2,)), dma((N_SPACE,)), dma((N_SPACE,))]
        + [dma((count, 2)), dma((count, 2)), dma((count,)), dma((count,)), dma((2,)), dma((2,))]
    )
    held = [(CX + 2, PY, NZ)] * 9 + [(3, CX + 4, 40, NZ)]
    given = (adjoint_state, forward_velocity, vp, shear_ratio, density, res, own, cells)
    given = [pltpu.with_memory_space_constraint(a, pltpu.HBM) for a in given]
    kept = pl.pallas_call(
        kernel,
        out_shape=tuple(pltpu.VMEM(shape, F32) for shape in held),
        in_specs=[hbm] * 8,
        out_specs=(vmem,) * len(held),
        scratch_shapes=scratch,
        compiler_params=pltpu.CompilerParams(collective_id=0, has_side_effects=True, vmem_limit_bytes=44 * 1024 * 1024),
    )(*given)
    kept = [pltpu.with_memory_space_constraint(a, pltpu.VMEM) for a in kept]
    return pl.pallas_call(
        finish,
        out_shape=(
            jax.ShapeDtypeStruct((1, 9, CX, NY, NZ), F32),
            jax.ShapeDtypeStruct((3, CX, 16, NZ), F32),
        ),
        in_specs=[vmem] * len(held),
        out_specs=(hbm, hbm),
        scratch_shapes=[pltpu.VMEM((3, CX + 4, 40, NZ), F32), pltpu.VMEM((3, CX, 16, NZ), F32), dma((10,))],
        compiler_params=pltpu.CompilerParams(vmem_limit_bytes=8 * 1024 * 1024),
    )(*kept)


def solution(mesh):
    in_specs = (
        P("shot", None, "space", None, None),
        P("shot", None, None, "space", None, None),
        P("space", None, None),
        P("space", None, None),
        P("space", None, None),
        P("shot", None, "space"),
        P("space", None),
        P("space"),
    )
    out_specs = (P("shot", None, "space", None, None), P(None, "space", "shot", None))
    return jax.shard_map(local, mesh=mesh, in_specs=in_specs, out_specs=out_specs, check_vma=False)
```

```python
import functools

import jax
import jax.numpy as jnp
from jax import lax
from jax.experimental import pallas as pl
from jax.experimental.pallas import tpu as pltpu
from jax.sharding import PartitionSpec as P

STEPS = 3
CX, NY, NZ = 16, 64, 128
NX = 512
N_SPACE = 32
CH_DEV = 1024
CAP = 128
COURANT = 0.3
KAPPA = 0.15
ROWS = 32
PAD = 8
PY = NY + 2 * PAD
VX, VY, VZ, SXX, SYY, SZZ, SXY, SXZ, SYZ = range(9)
GROUPS = ((3, 1), (0, 1), (7, 1), (1, 2), (5, 2), (4, 1))
F32, BF16, I32 = jnp.float32, jnp.bfloat16, jnp.int32


def nt(a, b):
    return lax.dot_general(a, b, (((1,), (1,)), ((), ())), preferred_element_type=F32)


def lane_of(rows):
    return lax.broadcasted_iota(I32, (rows, NZ), 1)


def zminus(f):
    rolled = pltpu.roll(f, 1, 1)
    return f - jnp.where(lane_of(f.shape[0]) == 0, 0.0, rolled)


def zplus(f):
    rolled = pltpu.roll(f, NZ - 1, 1)
    return jnp.where(lane_of(f.shape[0]) == NZ - 1, 0.0, rolled) - f


def kernel(
    adj, fwd, vp_h, sr_h, dn_h, res_h, own_h, cell_h,
    f0, f1, f2, f3, f4, f5, f6, f7, f8, h0,
    fw, dense, cb, cl, cm, g0, g1, g2,
    to_left, to_right, from_left, from_right, edge_b, rho_end,
    res, own, cell, packed, arrived, a_one, b_one,
    gs, rb1, s2, rb2,
    load_f, load_w, load_p, load_e, load_c,
    halo_s, halo_r, eb_s, eb_r, fh_s, fh_r, a2a_s, a2a_r,
    r1_s, r1_r, r2_s, r2_r, gx_s, gx_r,
):
    F = (f0, f1, f2, f3, f4, f5, f6, f7, f8)
    G = (g0, g1, g2)
    me = lax.axis_index("space")
    sh = lax.axis_index("shot")
    core = sh % 2
    chip = sh // 2
    has_left = me > 0
    has_right = me < N_SPACE - 1
    left = (me + N_SPACE - 1) % N_SPACE
    right = (me + 1) % N_SPACE
    mate = 2 * chip + (1 - core)
    cross = 2 * (1 - chip) + core
    inner = pl.ds(PAD, NY)

    ends = ((0, 0), (1, CX - 1))
    middle = pl.ds(1, CX - 2)
    loads_e = [pltpu.make_async_copy(dn_h.at[x], cb.at[x], load_e.at[9, i]) for i, x in ends]
    loads_e += [pltpu.make_async_copy(adj.at[0, k, x], F[k].at[x + 1, inner], load_e.at[k, i]) for k in range(9) for i, x in ends]
    loads_p = [pltpu.make_async_copy(vp_h, cl, load_p.at[0]), pltpu.make_async_copy(sr_h, cm, load_p.at[1])]
    loads_p.append(pltpu.make_async_copy(dn_h.at[middle], cb.at[middle], load_p.at[2]))
    loads_f = [pltpu.make_async_copy(adj.at[0, k, middle], F[k].at[pl.ds(2, CX - 2), inner], load_f.at[k]) for k in range(9)]
    loads_w = [pltpu.make_async_copy(fwd.at[0, t], fw.at[t, :, pl.ds(1, CX), inner], load_w.at[t]) for t in range(STEPS + 1)]
    loads_c = [pltpu.make_async_copy(src, dst, load_c.at[i]) for i, (src, dst) in enumerate(((own_h, own), (cell_h, cell), (res_h, res)))]
    for c in loads_c + loads_e + loads_p + loads_f + loads_w:
        c.start()

    zpad = jnp.zeros((PAD, NZ), F32)

    def zero_pads(x, carry):
        for k in (VX, VY, VZ, SYY, SXY, SYZ):
            F[k][x, pl.ds(0, PAD), :] = zpad
            F[k][x, pl.ds(PAD + NY, PAD), :] = zpad
        for t in range(STEPS):
            for k in range(3):
                fw[t, k, x, pl.ds(0, PAD), :] = zpad
                fw[t, k, x, pl.ds(PAD + NY, PAD), :] = zpad
        return carry

    lax.fori_loop(1, CX + 1, zero_pads, 0)

    def zero_h(x, carry):
        for k in range(3):
            h0[k, x, :, :] = jnp.zeros((40, NZ), F32)
        return carry

    lax.fori_loop(0, CX + 4, zero_h, 0)

    def zero_gs(i, carry):
        for k in range(3):
            for xx in range(2):
                gs[0, k, i, pl.ds(20 * xx, 2), :] = jnp.zeros((2, NZ), F32)
                gs[3, k, i, pl.ds(20 * xx + 18, 2), :] = jnp.zeros((2, NZ), F32)
        return carry

    lax.fori_loop(0, CX // 2, zero_gs, 0)
    zplane = jnp.zeros((NY, NZ), F32)

    @pl.when(me == 0)
    def _():
        edge_b[0] = zplane
        for t in range(STEPS):
            fw[t, 0, 0, inner, :] = zplane
            for k in range(3):
                from_left[t, k] = zplane

    @pl.when(me == N_SPACE - 1)
    def _():
        edge_b[1] = zplane
        for t in range(STEPS):
            for k in range(3):
                from_right[t, k] = zplane
            for k in (1, 2):
                fw[t, k, CX + 1, inner, :] = zplane

    barrier = pltpu.get_barrier_semaphore()

    def greet(k, carry):
        pl.semaphore_signal(barrier, inc=1, device_id={"space": (me + k) % N_SPACE}, device_id_type=pl.DeviceIdType.MESH)
        return carry

    lax.fori_loop(1, N_SPACE, greet, 0)
    for other in (mate, cross):
        pl.semaphore_signal(barrier, inc=1, device_id={"shot": other}, device_id_type=pl.DeviceIdType.MESH)

    def edges_out(step):
        for y in range(0, NY, ROWS):
            def at(k, x, dy=0):
                return F[k][x, pl.ds(PAD + y + dy, ROWS), :]

            rows = pl.ds(y, ROWS)
            b = cb[0, rows, :]
            syz = at(SYZ, 1)
            to_left[step, 0, rows, :] = at(SXX, 1)
            to_left[step, 1, rows, :] = at(VY, 1) + b * (at(SXY, 1) + (at(SYY, 1, 1) - at(SYY, 1)) + zminus(syz))
            to_left[step, 2, rows, :] = at(VZ, 1) + b * (at(SXZ, 1) + (syz - at(SYZ, 1, -1)) + zplus(at(SZZ, 1)))
            b = cb[CX - 1, rows, :]
            sxy, sxz = at(SXY, CX), at(SXZ, CX)
            to_right[step, 0, rows, :] = at(VX, CX) + b * ((sxy - at(SXY, CX, -1)) + zminus(sxz) - at(SXX, CX))
            to_right[step, 1, rows, :] = sxy
            to_right[step, 2, rows, :] = sxz

    def edges_in(step):
        for y in range(0, NY, ROWS):
            rows = pl.ds(y, ROWS)
            here = pl.ds(PAD + y, ROWS)
            b = edge_b[0, rows, :]
            F[VX][0, here, :] = from_left[step, 0, rows, :] + b * F[SXX][1, here, :]
            F[SXY][0, here, :] = from_left[step, 1, rows, :]
            F[SXZ][0, here, :] = from_left[step, 2, rows, :]
            b = edge_b[1, rows, :]
            F[SXX][CX + 1, here, :] = from_right[step, 0, rows, :]
            F[VY][CX + 1, here, :] = from_right[step, 1, rows, :] - b * F[SXY][CX, here, :]
            F[VZ][CX + 1, here, :] = from_right[step, 2, rows, :] - b * F[SXZ][CX, here, :]

    for c in loads_e:
        c.wait()
    for i, x in ends:
        rho = cb[x]
        rho_end[i] = rho
        cb[x] = COURANT * (1.0 / rho)
    edges_out(0)

    for c in loads_c:
        c.wait()
    blk = 256
    upper = (lax.broadcasted_iota(I32, (blk, blk), 0) < lax.broadcasted_iota(I32, (blk, blk), 1)).astype(F32).astype(BF16)
    carry_n = jnp.zeros((N_SPACE, 1), F32)
    acc = jnp.zeros((N_SPACE * 16, CAP), F32)
    for b in range(CH_DEV // blk):
        lanes = pl.ds(b * blk, blk)
        o = own[:, lanes]
        oh = (o == lax.broadcasted_iota(I32, (N_SPACE, blk), 0)).astype(F32)
        ranks = jnp.dot(oh.astype(BF16), upper, preferred_element_type=F32) + carry_n
        carry_n = carry_n + jnp.sum(oh, axis=1, keepdims=True)
        rank = jnp.sum(oh * ranks, axis=0, keepdims=True)
        slot = (rank.astype(I32) == lax.broadcasted_iota(I32, (CAP, blk), 0)).astype(F32).astype(BF16)
        cl_ = cell[:, lanes]
        r = [res[t, :, lanes] for t in range(STEPS)]
        hi = [v.astype(BF16).astype(F32) for v in r]
        zero = jnp.zeros((1, blk), F32)
        rows = (
            hi
            + [(cl_ >> 13).astype(F32), ((cl_ >> 7) & 63).astype(F32), (cl_ & 127).astype(F32), zero, zero]
            + [a - h for a, h in zip(r, hi)]
            + [zero] * 5
        )
        payload = jnp.concatenate(rows, axis=0)
        lhs = (oh[:, None, :] * payload[None, :, :]).reshape(N_SPACE * 16, blk).astype(BF16)
        acc = acc + nt(lhs, slot)
    acc = acc.reshape(N_SPACE, 16, CAP)
    packed[...] = acc[:, :8, :] + acc[:, 8:, :]

    pl.semaphore_wait(barrier, N_SPACE + 1)

    def send(src, dst, s, r, to):
        return pltpu.make_async_remote_copy(
            src_ref=src, dst_ref=dst, send_sem=s, recv_sem=r, device_id={"space": to}, device_id_type=pl.DeviceIdType.MESH
        )

    def edge_halo(step):
        return (
            [send(to_left.at[step], from_right.at[step], halo_s.at[step, 0], halo_r.at[step, 0], left)],
            [send(to_right.at[step], from_left.at[step], halo_s.at[step, 1], halo_r.at[step, 1], right)],
        )

    def density_halo():
        return (
            [send(dn_h.at[0], edge_b.at[1], eb_s.at[0], eb_r.at[0], left)],
            [send(dn_h.at[CX - 1], edge_b.at[0], eb_s.at[1], eb_r.at[1], right)],
        )

    def forward_halo():
        return (
            [send(fwd.at[0, pl.ds(0, STEPS), pl.ds(1, 2), 0], fw.at[pl.ds(0, STEPS), pl.ds(1, 2), CX + 1, inner], fh_s.at[0], fh_r.at[0], left)],
            [send(fwd.at[0, pl.ds(0, STEPS), 0, CX - 1], fw.at[pl.ds(0, STEPS), 0, 0, inner], fh_s.at[1], fh_r.at[1], right)],
        )

    def start(pair):
        @pl.when(has_left)
        def _():
            for c in pair[0]:
                c.start()

        @pl.when(has_right)
        def _():
            for c in pair[1]:
                c.start()

    def wait_recv(pair):
        @pl.when(has_right)
        def _():
            for c in pair[0]:
                c.wait_recv()

        @pl.when(has_left)
        def _():
            for c in pair[1]:
                c.wait_recv()

    def wait_send(pair):
        @pl.when(has_left)
        def _():
            for c in pair[0]:
                c.wait_send()

        @pl.when(has_right)
        def _():
            for c in pair[1]:
                c.wait_send()

    start(edge_halo(0))
    start(density_halo())

    def channel_copy(k):
        to = (me + k) % N_SPACE
        return send(packed.at[to], arrived.at[me], a2a_s.at[k], a2a_r.at[k], to)

    def channel_start(k, carry):
        channel_copy(k).start()
        return carry

    lax.fori_loop(1, N_SPACE, channel_start, 0)
    start(forward_halo())
    arrived[me] = packed[me]

    for c in loads_p:
        c.wait()

    def lame(x, rho):
        vp, ratio = cl[x], cm[x]
        vs = ratio * vp
        mu = rho * vs * vs
        cl[x] = COURANT * (rho * vp * vp - 2.0 * mu)
        cm[x] = COURANT * mu

    def params(x, carry):
        rho = cb[x]
        cb[x] = COURANT * (1.0 / rho)
        lame(x, rho)
        return carry

    lax.fori_loop(1, CX - 1, params, 0)
    for i, x in ends:
        lame(x, rho_end[i])
    for c in loads_f:
        c.wait()

    def speeds(x, carry=0):
        for y in range(0, NY, ROWS):
            def at(k, dx=0, dy=0):
                return F[k][x + dx, pl.ds(PAD + y + dy, ROWS), :]

            here = pl.ds(PAD + y, ROWS)
            b = cb[x - 1, pl.ds(y, ROWS), :]
            sxy, sxz, syz = at(SXY), at(SXZ), at(SYZ)
            vx = at(VX) + b * ((at(SXX, 1) - at(SXX)) + (sxy - at(SXY, 0, -1)) + zminus(sxz))
            vy = at(VY) + b * ((sxy - at(SXY, -1)) + (at(SYY, 0, 1) - at(SYY)) + zminus(syz))
            vz = at(VZ) + b * ((sxz - at(SXZ, -1)) + (syz - at(SYZ, 0, -1)) + zplus(at(SZZ)))
            F[VX][x, here, :] = vx
            F[VY][x, here, :] = vy
            F[VZ][x, here, :] = vz
        return carry

    def stresses(step, x, carry=0):
        inject = step > 0
        for y in range(0, NY, ROWS):
            def at(k, dx=0, dy=0):
                return F[k][x + dx, pl.ds(PAD + y + dy, ROWS), :]

            here = pl.ds(PAD + y, ROWS)
            flat = pl.ds(y, ROWS)
            lam, mu = cl[x - 1, flat, :], cm[x - 1, flat, :]
            vx, vy, vz = at(VX), at(VY), at(VZ)
            exx = vx - at(VX, -1)
            eyy = vy - at(VY, 0, -1)
            ezz = zminus(vz)
            base = lam * (exx + eyy + ezz)
            mu2 = mu + mu
            F[SXX][x, here, :] = at(SXX) + (base + mu2 * exx)
            F[SYY][x, here, :] = at(SYY) + (base + mu2 * eyy)
            szz = at(SZZ) + (base + mu2 * ezz)
            F[SZZ][x, here, :] = szz + dense[step, x - 1, flat, :] if inject else szz
            F[SXY][x, here, :] = at(SXY) + mu * ((at(VY, 1) - vy) + (at(VX, 0, 1) - vx))
            F[SXZ][x, here, :] = at(SXZ) + mu * ((at(VZ, 1) - vz) + zplus(vx))
            F[SYZ][x, here, :] = at(SYZ) + mu * ((at(VZ, 0, 1) - vz) + zplus(vy))
        return carry

    def gradients(step, x, carry=0):
        for y in range(0, NY, ROWS):
            def at(k):
                return F[k][x, pl.ds(PAD + y, ROWS), :]

            def u(k, dx=0, dy=0):
                return fw[step, k, x + dx, pl.ds(PAD + y + dy, ROWS), :]

            def w(k):
                return fw[step + 1, k, x, pl.ds(PAD + y, ROWS), :]

            flat = pl.ds(y, ROWS)
            sxx, syy, szz = at(SXX), at(SYY), at(SZZ)
            ux, uy, uz = u(0), u(1), u(2)
            fxx = ux - u(0, -1)
            fyy = uy - u(1, 0, -1)
            fzz = zminus(uz)
            lam = (fxx + fyy + fzz) * (sxx + syy + szz)
            mu = (
                2.0 * (fxx * sxx + fyy * syy + fzz * szz)
                + ((u(1, 1) - uy) + (u(0, 0, 1) - ux)) * at(SXY)
                + ((u(2, 1) - uz) + zplus(ux)) * at(SXZ)
                + ((u(2, 0, 1) - uz) + zplus(uy)) * at(SYZ)
            )
            rho = at(VX) * (w(0) - ux) + at(VY) * (w(1) - uy) + at(VZ) * (w(2) - uz)
            for ref, term in zip(G, (lam, mu, rho)):
                ref[x - 1, flat, :] = term if step == 0 else ref[x - 1, flat, :] + term
        return carry

    def densify():
        def channel_wait(k, carry):
            channel_copy(k).wait_recv()
            return carry

        lax.fori_loop(1, N_SPACE, channel_wait, 0)

        def one_hot(s, carry):
            row = arrived[s]
            x, y, z = row[3:4].astype(I32), row[4:5].astype(I32), row[5:6].astype(I32)

            def tile(v):
                return jnp.broadcast_to(v, (16, CAP)).astype(BF16)

            yone = (y == lax.broadcasted_iota(I32, (NY, CAP), 0)).astype(F32).astype(BF16)
            zone = (z == lax.broadcasted_iota(I32, (NZ, CAP), 0)).astype(F32).astype(BF16)
            yone, zone = yone.reshape(NY // 16, 16, CAP), zone.reshape(NZ // 16, 16, CAP)
            for i in range(CX):
                xone = tile((x == i).astype(F32))
                a_one[s, pl.ds(i * NY, NY), :] = (yone * xone[None]).reshape(NY, CAP)
            for t in range(STEPS):
                v = row[t : t + 1]
                hi = v.astype(BF16).astype(F32)
                b_one[t, s, pl.ds(0, NZ), :] = (zone * tile(hi)[None]).reshape(NZ, CAP)
                b_one[t, s, pl.ds(NZ, NZ), :] = (zone * tile(v - hi)[None]).reshape(NZ, CAP)
            return carry

        lax.fori_loop(0, N_SPACE, one_hot, 0)

    def product(m, t):
        rows = pl.ds(pl.multiple_of(m * 256, 256), 256)
        got = nt(
            jnp.concatenate([a_one[s, rows, :] for s in range(N_SPACE)], axis=1),
            jnp.concatenate([b_one[t, s] for s in range(N_SPACE)], axis=1),
        )
        dense[t, pl.ds(4 * m, 4), :, :] = (got[:, :NZ] + got[:, NZ:]).reshape(4, NY, NZ)

    def first_product(m, carry):
        product(m, 0)
        for i in range(4):
            x = 4 * m + i + 1
            F[SZZ][x, inner, :] = F[SZZ][x, inner, :] + dense[0, x - 1]
        return carry

    def later_products(m, carry):
        for t in range(1, STEPS):
            product(m, t)
        for i in range(4):
            gradients(0, 4 * m + i + 1)
        return carry

    def end_planes(step):
        edges_in(step)
        speeds(1)
        speeds(CX)

    lax.fori_loop(2, CX, speeds, 0)
    lax.fori_loop(3, CX - 1, functools.partial(stresses, 0), 0)
    wait_recv(edge_halo(0))
    wait_recv(density_halo())
    for i in range(2):
        @pl.when(has_left if i == 0 else has_right)
        def _():
            edge_b[i] = COURANT * (1.0 / edge_b[i])
    end_planes(0)
    for x in (1, 2, CX - 1, CX):
        stresses(0, x)
    densify()
    lax.fori_loop(0, 4, first_product, 0)
    edges_out(1)
    start(edge_halo(1))
    for c in loads_w:
        c.wait()
    wait_recv(forward_halo())
    lax.fori_loop(0, 4, later_products, 0)

    lax.fori_loop(2, CX, speeds, 0)
    wait_recv(edge_halo(1))
    end_planes(1)
    stresses(1, 1)
    stresses(1, CX)
    edges_out(2)
    start(edge_halo(2))
    lax.fori_loop(2, CX, functools.partial(stresses, 1), 0)
    lax.fori_loop(1, CX + 1, functools.partial(gradients, 1), 0)

    lax.fori_loop(2, CX, speeds, 0)

    def to_mate(n):
        pairs = pl.ds(*GROUPS[n])
        return [
            pltpu.make_async_remote_copy(
                src_ref=gs.at[2 * j + 1 - core, :, pairs],
                dst_ref=rb1.at[j, :, pairs],
                send_sem=r1_s.at[n, j],
                recv_sem=r1_r.at[n, j],
                device_id={"shot": mate},
                device_id_type=pl.DeviceIdType.MESH,
            )
            for j in range(2)
        ]

    def to_cross(n):
        pairs = pl.ds(*GROUPS[n])
        return pltpu.make_async_remote_copy(
            src_ref=s2.at[:, pairs],
            dst_ref=rb2.at[:, pairs],
            send_sem=r2_s.at[n],
            recv_sem=r2_r.at[n],
            device_id={"shot": cross},
            device_id_type=pl.DeviceIdType.MESH,
        )

    def pairs_of(n, body):
        first, count = GROUPS[n]
        lax.fori_loop(first, first + count, body, 0)

    def slabs(i, carry):
        for k in range(3):
            for xx in range(2):
                for s in range(4):
                    lo, hi = max(0, 16 * s - 2), min(NY, 16 * s + 18)
                    off = 20 * xx + lo - (16 * s - 2)
                    gs[s, k, i, pl.ds(off, hi - lo), :] = G[k][2 * i + xx, pl.ds(lo, hi - lo), :]
        return carry

    def sum_cross(i, carry):
        for k in range(3):
            s2[k, i] = gs[2 * (1 - chip) + core, k, i] + rb1[1 - chip, k, i]
        return carry

    def pass_on(n):
        for c in to_mate(n):
            c.wait_recv()
        pairs_of(n, sum_cross)
        to_cross(n).start()

    def last(x, carry):
        stresses(STEPS - 1, x)
        gradients(STEPS - 1, x)
        return carry

    for n, (first, count) in enumerate(GROUPS):
        if n == 1:
            wait_recv(edge_halo(2))
            end_planes(2)
        lax.fori_loop(2 * first + 1, 2 * (first + count) + 1, last, 0)
        pairs_of(n, slabs)
        for c in to_mate(n):
            c.start()
        if n > 0:
            pass_on(n - 1)
    pass_on(len(GROUPS) - 1)

    def sum_own(i, carry):
        for k in range(3):
            for xx in range(2):
                part = pl.ds(20 * xx, 20)
                total = (gs[2 * chip + core, k, i, part, :] + rb1[chip, k, i, part, :]) + rb2[k, i, part, :]
                h0[k, 2 + 2 * i + xx, pl.ds(8, 20), :] = total
        return carry

    rim = pl.ds(8, 24)
    grad_halo = (
        [send(h0.at[:, pl.ds(2, 2), rim], h0.at[:, pl.ds(CX + 2, 2), rim], gx_s.at[0], gx_r.at[0], left)],
        [send(h0.at[:, pl.ds(CX, 2), rim], h0.at[:, pl.ds(0, 2), rim], gx_s.at[1], gx_r.at[1], right)],
    )
    for n in range(len(GROUPS)):
        to_cross(n).wait_recv()
        pairs_of(n, sum_own)
        if n == 2:
            start(grad_halo)
    wait_recv(grad_halo)
    wait_send(grad_halo)

    for step in range(STEPS):
        wait_send(edge_halo(step))
    wait_send(density_halo())
    wait_send(forward_halo())

    def channel_sent(k, carry):
        channel_copy(k).wait_send()
        return carry

    lax.fori_loop(1, N_SPACE, channel_sent, 0)
    for n in range(len(GROUPS)):
        for c in to_mate(n):
            c.wait_send()
        to_cross(n).wait_send()


def finish(f0, f1, f2, f3, f4, f5, f6, f7, f8, h0, out_adj, out_grad, h1, og, sem):
    me = lax.axis_index("space")
    sh = lax.axis_index("shot")
    fields = (f0, f1, f2, f3, f4, f5, f6, f7, f8)
    stores = [pltpu.make_async_copy(f.at[pl.ds(1, CX), pl.ds(PAD, NY)], out_adj.at[0, k], sem.at[k]) for k, f in enumerate(fields)]
    for c in stores:
        c.start()

    def near(h, k, p, lo, n):
        def at(dp=0, dy=0):
            return h[k, p + dp, pl.ds(lo + dy, n), :]

        mid = at()
        lane = lane_of(n)
        total = at(1) + at(-1) + at(0, 1) + at(0, -1)
        total = total + jnp.where(lane == NZ - 1, 0.0, pltpu.roll(mid, NZ - 1, 1)) + jnp.where(lane == 0, 0.0, pltpu.roll(mid, 1, 1))
        return mid + KAPPA * (total - 6.0 * mid)

    def sweep_one(p, carry):
        gx = CX * me + p - 2
        gy = 16 * sh - 2 + lax.broadcasted_iota(I32, (24, NZ), 0)
        keep = (gy >= 0) & (gy < NY) & (gx >= 0) & (gx < NX)
        for k in range(3):
            h1[k, p, pl.ds(8, 24), :] = jnp.where(keep, near(h0, k, p, 8, 24), 0.0)
        return carry

    lax.fori_loop(1, CX + 3, sweep_one, 0)

    def sweep_two(x, carry):
        for k in range(3):
            og[k, x] = near(h1, k, x + 2, 10, 16)
        return carry

    lax.fori_loop(0, CX, sweep_two, 0)
    grad_out = pltpu.make_async_copy(og, out_grad, sem.at[9])
    grad_out.start()
    grad_out.wait()
    for c in stores:
        c.wait()


def local(adjoint_state, forward_velocity, vp, shear_ratio, density, residuals, owner, cell):
    res = residuals.reshape(STEPS, 1, CH_DEV)
    own = owner.reshape(1, CH_DEV)
    cells = cell.reshape(1, CH_DEV)
    hbm = pl.BlockSpec(memory_space=pltpu.HBM)
    vmem = pl.BlockSpec(memory_space=pltpu.VMEM)
    volume = pltpu.VMEM((CX, NY, NZ), F32)
    dma = pltpu.SemaphoreType.DMA
    edges = pltpu.VMEM((STEPS, 3, NY, NZ), F32)
    pair = pltpu.VMEM((2, NY, NZ), F32)
    count = len(GROUPS)
    scratch = (
        [
            pltpu.VMEM((STEPS + 1, 3, CX + 2, PY, NZ), F32),
            pltpu.VMEM((STEPS, CX, NY, NZ), F32),
        ]
        + [volume] * 6
        + [edges] * 4
        + [pair] * 2
        + [
            pltpu.VMEM((STEPS, 1, CH_DEV), F32),
            pltpu.VMEM((1, CH_DEV), I32),
            pltpu.VMEM((1, CH_DEV), I32),
            pltpu.VMEM((N_SPACE, 8, CAP), F32),
            pltpu.VMEM((N_SPACE, 8, CAP), F32),
            pltpu.VMEM((N_SPACE, CX * NY, CAP), BF16),
            pltpu.VMEM((STEPS, N_SPACE, 2 * NZ, CAP), BF16),
            pltpu.VMEM((4, 3, CX // 2, 40, NZ), F32),
            pltpu.VMEM((2, 3, CX // 2, 40, NZ), F32),
            pltpu.VMEM((3, CX // 2, 40, NZ), F32),
            pltpu.VMEM((3, CX // 2, 40, NZ), F32),
        ]
        + [dma((9,)), dma((4,)), dma((3,)), dma((10, 2)), dma((3,))]
        + [dma((STEPS, 2)), dma((STEPS, 2)), dma((2,)), dma((2,)), dma((2,)), dma((2,)), dma((N_SPACE,)), dma((N_SPACE,))]
        + [dma((count, 2)), dma((count, 2)), dma((count,)), dma((count,)), dma((2,)), dma((2,))]
    )
    held = [(CX + 2, PY, NZ)] * 9 + [(3, CX + 4, 40, NZ)]
    given = (adjoint_state, forward_velocity, vp, shear_ratio, density, res, own, cells)
    given = [pltpu.with_memory_space_constraint(a, pltpu.HBM) for a in given]
    kept = pl.pallas_call(
        kernel,
        out_shape=tuple(pltpu.VMEM(shape, F32) for shape in held),
        in_specs=[hbm] * 8,
        out_specs=(vmem,) * len(held),
        scratch_shapes=scratch,
        compiler_params=pltpu.CompilerParams(collective_id=0, has_side_effects=True, vmem_limit_bytes=44 * 1024 * 1024),
    )(*given)
    kept = [pltpu.with_memory_space_constraint(a, pltpu.VMEM) for a in kept]
    return pl.pallas_call(
        finish,
        out_shape=(
            jax.ShapeDtypeStruct((1, 9, CX, NY, NZ), F32),
            jax.ShapeDtypeStruct((3, CX, 16, NZ), F32),
        ),
        in_specs=[vmem] * len(held),
        out_specs=(hbm, hbm),
        scratch_shapes=[pltpu.VMEM((3, CX + 4, 40, NZ), F32), pltpu.VMEM((3, CX, 16, NZ), F32), dma((10,))],
        compiler_params=pltpu.CompilerParams(vmem_limit_bytes=8 * 1024 * 1024),
    )(*kept)


def solution(mesh):
    in_specs = (
        P("shot", None, "space", None, None),
        P("shot", None, None, "space", None, None),
        P("space", None, None),
        P("space", None, None),
        P("space", None, None),
        P("shot", None, "space"),
        P("space", None),
        P("space"),
    )
    out_specs = (P("shot", None, "space", None, None), P(None, "space", "shot", None))
    return jax.shard_map(local, mesh=mesh, in_specs=in_specs, out_specs=out_specs, check_vma=False)
```

```python
import functools

import jax
import jax.numpy as jnp
from jax import lax
from jax.experimental import pallas as pl
from jax.experimental.pallas import tpu as pltpu
from jax.sharding import PartitionSpec as P

STEPS = 3
CX, NY, NZ = 16, 64, 128
NX = 512
N_SPACE = 32
CH_DEV = 1024
CAP = 128
COURANT = 0.3
KAPPA = 0.15
ROWS = 32
PAD = 8
PY = NY + 2 * PAD
VX, VY, VZ, SXX, SYY, SZZ, SXY, SXZ, SYZ = range(9)
GROUPS = ((3, 2), (0, 1), (7, 1), (1, 2), (5, 2))
F32, BF16, I32 = jnp.float32, jnp.bfloat16, jnp.int32


def nt(a, b):
    return lax.dot_general(a, b, (((1,), (1,)), ((), ())), preferred_element_type=F32)


def lane_of(rows):
    return lax.broadcasted_iota(I32, (rows, NZ), 1)


def zminus(f):
    rolled = pltpu.roll(f, 1, 1)
    return f - jnp.where(lane_of(f.shape[0]) == 0, 0.0, rolled)


def zplus(f):
    rolled = pltpu.roll(f, NZ - 1, 1)
    return jnp.where(lane_of(f.shape[0]) == NZ - 1, 0.0, rolled) - f


def kernel(
    adj, fwd, vp_h, sr_h, dn_h, res_h, own_h, cell_h,
    f0, f1, f2, f3, f4, f5, f6, f7, f8, h0,
    fw, dense, cb, cl, cm, g0, g1, g2,
    to_left, to_right, from_left, from_right, edge_b, rho_end,
    res, own, cell, packed, arrived, a_one, b_one,
    gs, rb1, s2, rb2,
    load_f, load_w, load_p, load_e, load_c,
    halo_s, halo_r, eb_s, eb_r, fh_s, fh_r, a2a_s, a2a_r,
    r1_s, r1_r, r2_s, r2_r, gx_s, gx_r,
):
    F = (f0, f1, f2, f3, f4, f5, f6, f7, f8)
    G = (g0, g1, g2)
    me = lax.axis_index("space")
    sh = lax.axis_index("shot")
    core = sh % 2
    chip = sh // 2
    has_left = me > 0
    has_right = me < N_SPACE - 1
    left = (me + N_SPACE - 1) % N_SPACE
    right = (me + 1) % N_SPACE
    mate = 2 * chip + (1 - core)
    cross = 2 * (1 - chip) + core
    inner = pl.ds(PAD, NY)

    ends = ((0, 0), (1, CX - 1))
    middle = pl.ds(1, CX - 2)
    loads_e = [pltpu.make_async_copy(dn_h.at[x], cb.at[x], load_e.at[9, i]) for i, x in ends]
    loads_e += [pltpu.make_async_copy(adj.at[0, k, x], F[k].at[x + 1, inner], load_e.at[k, i]) for k in range(9) for i, x in ends]
    loads_p = [pltpu.make_async_copy(vp_h, cl, load_p.at[0]), pltpu.make_async_copy(sr_h, cm, load_p.at[1])]
    loads_p.append(pltpu.make_async_copy(dn_h.at[middle], cb.at[middle], load_p.at[2]))
    loads_f = [pltpu.make_async_copy(adj.at[0, k, middle], F[k].at[pl.ds(2, CX - 2), inner], load_f.at[k]) for k in range(9)]
    loads_w = [pltpu.make_async_copy(fwd.at[0, t], fw.at[t, :, pl.ds(1, CX), inner], load_w.at[t]) for t in range(STEPS + 1)]
    loads_c = [pltpu.make_async_copy(src, dst, load_c.at[i]) for i, (src, dst) in enumerate(((own_h, own), (cell_h, cell), (res_h, res)))]
    for c in loads_e + loads_c + loads_f + loads_p + loads_w:
        c.start()

    barrier = pltpu.get_barrier_semaphore()

    def greet(k, carry):
        pl.semaphore_signal(barrier, inc=1, device_id={"space": (me + k) % N_SPACE}, device_id_type=pl.DeviceIdType.MESH)
        return carry

    for other in (mate, cross):
        pl.semaphore_signal(barrier, inc=1, device_id={"shot": other}, device_id_type=pl.DeviceIdType.MESH)
    lax.fori_loop(1, N_SPACE, greet, 0)

    zpad = jnp.zeros((PAD, NZ), F32)

    def zero_pads(x, carry):
        for k in (VX, VY, VZ, SYY, SXY, SYZ):
            F[k][x, pl.ds(0, PAD), :] = zpad
            F[k][x, pl.ds(PAD + NY, PAD), :] = zpad
        for t in range(STEPS):
            for k in range(3):
                fw[t, k, x, pl.ds(0, PAD), :] = zpad
                fw[t, k, x, pl.ds(PAD + NY, PAD), :] = zpad
        return carry

    zero_pads(1, 0)
    zero_pads(CX, 0)
    zplane = jnp.zeros((NY, NZ), F32)

    @pl.when(me == 0)
    def _():
        edge_b[0] = zplane
        for t in range(STEPS):
            fw[t, 0, 0, inner, :] = zplane
            for k in range(3):
                from_left[t, k] = zplane

    @pl.when(me == N_SPACE - 1)
    def _():
        edge_b[1] = zplane
        for t in range(STEPS):
            for k in range(3):
                from_right[t, k] = zplane
            for k in (1, 2):
                fw[t, k, CX + 1, inner, :] = zplane

    def edges_out(step):
        for y in range(0, NY, ROWS):
            def at(k, x, dy=0):
                return F[k][x, pl.ds(PAD + y + dy, ROWS), :]

            rows = pl.ds(y, ROWS)
            b = cb[0, rows, :]
            syz = at(SYZ, 1)
            to_left[step, 0, rows, :] = at(SXX, 1)
            to_left[step, 1, rows, :] = at(VY, 1) + b * (at(SXY, 1) + (at(SYY, 1, 1) - at(SYY, 1)) + zminus(syz))
            to_left[step, 2, rows, :] = at(VZ, 1) + b * (at(SXZ, 1) + (syz - at(SYZ, 1, -1)) + zplus(at(SZZ, 1)))
            b = cb[CX - 1, rows, :]
            sxy, sxz = at(SXY, CX), at(SXZ, CX)
            to_right[step, 0, rows, :] = at(VX, CX) + b * ((sxy - at(SXY, CX, -1)) + zminus(sxz) - at(SXX, CX))
            to_right[step, 1, rows, :] = sxy
            to_right[step, 2, rows, :] = sxz

    def edges_in(step):
        for y in range(0, NY, ROWS):
            rows = pl.ds(y, ROWS)
            here = pl.ds(PAD + y, ROWS)
            b = edge_b[0, rows, :]
            F[VX][0, here, :] = from_left[step, 0, rows, :] + b * F[SXX][1, here, :]
            F[SXY][0, here, :] = from_left[step, 1, rows, :]
            F[SXZ][0, here, :] = from_left[step, 2, rows, :]
            b = edge_b[1, rows, :]
            F[SXX][CX + 1, here, :] = from_right[step, 0, rows, :]
            F[VY][CX + 1, here, :] = from_right[step, 1, rows, :] - b * F[SXY][CX, here, :]
            F[VZ][CX + 1, here, :] = from_right[step, 2, rows, :] - b * F[SXZ][CX, here, :]

    for c in loads_e:
        c.wait()
    for i, x in ends:
        rho = cb[x]
        rho_end[i] = rho
        cb[x] = COURANT * (1.0 / rho)
    edges_out(0)

    pl.semaphore_wait(barrier, N_SPACE + 1)

    def send(src, dst, s, r, to):
        return pltpu.make_async_remote_copy(
            src_ref=src, dst_ref=dst, send_sem=s, recv_sem=r, device_id={"space": to}, device_id_type=pl.DeviceIdType.MESH
        )

    def edge_halo(step):
        return (
            [send(to_left.at[step], from_right.at[step], halo_s.at[step, 0], halo_r.at[step, 0], left)],
            [send(to_right.at[step], from_left.at[step], halo_s.at[step, 1], halo_r.at[step, 1], right)],
        )

    def density_halo():
        return (
            [send(dn_h.at[0], edge_b.at[1], eb_s.at[0], eb_r.at[0], left)],
            [send(dn_h.at[CX - 1], edge_b.at[0], eb_s.at[1], eb_r.at[1], right)],
        )

    def forward_halo():
        return (
            [send(fwd.at[0, pl.ds(0, STEPS), pl.ds(1, 2), 0], fw.at[pl.ds(0, STEPS), pl.ds(1, 2), CX + 1, inner], fh_s.at[0], fh_r.at[0], left)],
            [send(fwd.at[0, pl.ds(0, STEPS), 0, CX - 1], fw.at[pl.ds(0, STEPS), 0, 0, inner], fh_s.at[1], fh_r.at[1], right)],
        )

    def start(pair):
        @pl.when(has_left)
        def _():
            for c in pair[0]:
                c.start()

        @pl.when(has_right)
        def _():
            for c in pair[1]:
                c.start()

    def wait_recv(pair):
        @pl.when(has_right)
        def _():
            for c in pair[0]:
                c.wait_recv()

        @pl.when(has_left)
        def _():
            for c in pair[1]:
                c.wait_recv()

    def wait_send(pair):
        @pl.when(has_left)
        def _():
            for c in pair[0]:
                c.wait_send()

        @pl.when(has_right)
        def _():
            for c in pair[1]:
                c.wait_send()

    start(edge_halo(0))
    start(density_halo())

    for c in loads_c:
        c.wait()
    blk = 256
    upper = (lax.broadcasted_iota(I32, (blk, blk), 0) < lax.broadcasted_iota(I32, (blk, blk), 1)).astype(F32).astype(BF16)
    carry_n = jnp.zeros((N_SPACE, 1), F32)
    acc = jnp.zeros((N_SPACE * 16, CAP), F32)
    for b in range(CH_DEV // blk):
        lanes = pl.ds(b * blk, blk)
        o = own[:, lanes]
        oh = (o == lax.broadcasted_iota(I32, (N_SPACE, blk), 0)).astype(F32)
        ranks = jnp.dot(oh.astype(BF16), upper, preferred_element_type=F32) + carry_n
        carry_n = carry_n + jnp.sum(oh, axis=1, keepdims=True)
        rank = jnp.sum(oh * ranks, axis=0, keepdims=True)
        slot = (rank.astype(I32) == lax.broadcasted_iota(I32, (CAP, blk), 0)).astype(F32).astype(BF16)
        cl_ = cell[:, lanes]
        r = [res[t, :, lanes] for t in range(STEPS)]
        hi = [v.astype(BF16).astype(F32) for v in r]
        zero = jnp.zeros((1, blk), F32)
        rows = (
            hi
            + [(cl_ >> 13).astype(F32), ((cl_ >> 7) & 63).astype(F32), (cl_ & 127).astype(F32), zero, zero]
            + [a - h for a, h in zip(r, hi)]
            + [zero] * 5
        )
        payload = jnp.concatenate(rows, axis=0)
        lhs = (oh[:, None, :] * payload[None, :, :]).reshape(N_SPACE * 16, blk).astype(BF16)
        acc = acc + nt(lhs, slot)
    acc = acc.reshape(N_SPACE, 16, CAP)
    packed[...] = acc[:, :8, :] + acc[:, 8:, :]

    def channel_copy(k):
        to = (me + k) % N_SPACE
        return send(packed.at[to], arrived.at[me], a2a_s.at[k], a2a_r.at[k], to)

    def channel_start(k, carry):
        channel_copy(k).start()
        return carry

    lax.fori_loop(1, N_SPACE, channel_start, 0)
    start(forward_halo())
    arrived[me] = packed[me]

    lax.fori_loop(2, CX, zero_pads, 0)

    def zero_h(x, carry):
        for k in range(3):
            h0[k, x, :, :] = jnp.zeros((40, NZ), F32)
        return carry

    lax.fori_loop(0, CX + 4, zero_h, 0)

    def zero_gs(i, carry):
        for k in range(3):
            for xx in range(2):
                gs[0, k, i, pl.ds(20 * xx, 2), :] = jnp.zeros((2, NZ), F32)
                gs[3, k, i, pl.ds(20 * xx + 18, 2), :] = jnp.zeros((2, NZ), F32)
        return carry

    lax.fori_loop(0, CX // 2, zero_gs, 0)

    for c in loads_p:
        c.wait()

    def lame(x, rho):
        vp, ratio = cl[x], cm[x]
        vs = ratio * vp
        mu = rho * vs * vs
        cl[x] = COURANT * (rho * vp * vp - 2.0 * mu)
        cm[x] = COURANT * mu

    def params(x, carry):
        rho = cb[x]
        cb[x] = COURANT * (1.0 / rho)
        lame(x, rho)
        return carry

    lax.fori_loop(1, CX - 1, params, 0)
    for i, x in ends:
        lame(x, rho_end[i])
    for c in loads_f:
        c.wait()

    def speeds(x, carry=0):
        for y in range(0, NY, ROWS):
            def at(k, dx=0, dy=0):
                return F[k][x + dx, pl.ds(PAD + y + dy, ROWS), :]

            here = pl.ds(PAD + y, ROWS)
            b = cb[x - 1, pl.ds(y, ROWS), :]
            sxy, sxz, syz = at(SXY), at(SXZ), at(SYZ)
            vx = at(VX) + b * ((at(SXX, 1) - at(SXX)) + (sxy - at(SXY, 0, -1)) + zminus(sxz))
            vy = at(VY) + b * ((sxy - at(SXY, -1)) + (at(SYY, 0, 1) - at(SYY)) + zminus(syz))
            vz = at(VZ) + b * ((sxz - at(SXZ, -1)) + (syz - at(SYZ, 0, -1)) + zplus(at(SZZ)))
            F[VX][x, here, :] = vx
            F[VY][x, here, :] = vy
            F[VZ][x, here, :] = vz
        return carry

    def stresses(step, x, carry=0, add=False):
        for y in range(0, NY, ROWS):
            def at(k, dx=0, dy=0):
                return F[k][x + dx, pl.ds(PAD + y + dy, ROWS), :]

            here = pl.ds(PAD + y, ROWS)
            flat = pl.ds(y, ROWS)
            lam, mu = cl[x - 1, flat, :], cm[x - 1, flat, :]
            vx, vy, vz = at(VX), at(VY), at(VZ)
            exx = vx - at(VX, -1)
            eyy = vy - at(VY, 0, -1)
            ezz = zminus(vz)
            base = lam * (exx + eyy + ezz)
            mu2 = mu + mu
            szz = at(SZZ) + (base + mu2 * ezz)
            new = [
                at(SXX) + (base + mu2 * exx),
                at(SYY) + (base + mu2 * eyy),
                szz + dense[step, x - 1, flat, :] if step > 0 else szz,
                at(SXY) + mu * ((at(VY, 1) - vy) + (at(VX, 0, 1) - vx)),
                at(SXZ) + mu * ((at(VZ, 1) - vz) + zplus(vx)),
                at(SYZ) + mu * ((at(VZ, 0, 1) - vz) + zplus(vy)),
            ]
            for k, v in zip((SXX, SYY, SZZ, SXY, SXZ, SYZ), new):
                F[k][x, here, :] = v
            if add:
                add_terms(step, x, y, vx, vy, vz, *new)
        return carry

    def add_terms(step, x, y, vx, vy, vz, sxx, syy, szz, sxy, sxz, syz):
        def u(k, dx=0, dy=0):
            return fw[step, k, x + dx, pl.ds(PAD + y + dy, ROWS), :]

        def w(k):
            return fw[step + 1, k, x, pl.ds(PAD + y, ROWS), :]

        flat = pl.ds(y, ROWS)
        ux, uy, uz = u(0), u(1), u(2)
        fxx = ux - u(0, -1)
        fyy = uy - u(1, 0, -1)
        fzz = zminus(uz)
        lam = (fxx + fyy + fzz) * (sxx + syy + szz)
        mu = (
            2.0 * (fxx * sxx + fyy * syy + fzz * szz)
            + ((u(1, 1) - uy) + (u(0, 0, 1) - ux)) * sxy
            + ((u(2, 1) - uz) + zplus(ux)) * sxz
            + ((u(2, 0, 1) - uz) + zplus(uy)) * syz
        )
        rho = vx * (w(0) - ux) + vy * (w(1) - uy) + vz * (w(2) - uz)
        for ref, term in zip(G, (lam, mu, rho)):
            ref[x - 1, flat, :] = term if step == 0 else ref[x - 1, flat, :] + term

    def gradients(step, x, carry=0):
        for y in range(0, NY, ROWS):
            add_terms(step, x, y, *[F[k][x, pl.ds(PAD + y, ROWS), :] for k in range(9)])
        return carry

    def densify():
        def channel_wait(k, carry):
            channel_copy(k).wait_recv()
            return carry

        lax.fori_loop(1, N_SPACE, channel_wait, 0)

        def one_hot(s, carry):
            row = arrived[s]
            x, y, z = row[3:4].astype(I32), row[4:5].astype(I32), row[5:6].astype(I32)

            def tile(v):
                return jnp.broadcast_to(v, (16, CAP)).astype(BF16)

            yone = (y == lax.broadcasted_iota(I32, (NY, CAP), 0)).astype(F32).astype(BF16)
            zone = (z == lax.broadcasted_iota(I32, (NZ, CAP), 0)).astype(F32).astype(BF16)
            yone, zone = yone.reshape(NY // 16, 16, CAP), zone.reshape(NZ // 16, 16, CAP)
            for i in range(CX):
                xone = tile((x == i).astype(F32))
                a_one[s, pl.ds(i * NY, NY), :] = (yone * xone[None]).reshape(NY, CAP)
            for t in range(STEPS):
                v = row[t : t + 1]
                hi = v.astype(BF16).astype(F32)
                b_one[t, s, pl.ds(0, NZ), :] = (zone * tile(hi)[None]).reshape(NZ, CAP)
                b_one[t, s, pl.ds(NZ, NZ), :] = (zone * tile(v - hi)[None]).reshape(NZ, CAP)
            return carry

        lax.fori_loop(0, N_SPACE, one_hot, 0)

    def product(m, t):
        rows = pl.ds(pl.multiple_of(m * 256, 256), 256)
        got = nt(
            jnp.concatenate([a_one[s, rows, :] for s in range(N_SPACE)], axis=1),
            jnp.concatenate([b_one[t, s] for s in range(N_SPACE)], axis=1),
        )
        dense[t, pl.ds(4 * m, 4), :, :] = (got[:, :NZ] + got[:, NZ:]).reshape(4, NY, NZ)

    def first_product(m, carry):
        product(m, 0)
        for i in range(4):
            x = 4 * m + i + 1
            F[SZZ][x, inner, :] = F[SZZ][x, inner, :] + dense[0, x - 1]
        return carry

    def later_products(m, carry):
        for t in range(1, STEPS):
            product(m, t)
        for i in range(4):
            gradients(0, 4 * m + i + 1)
        return carry

    def end_planes(step):
        edges_in(step)
        speeds(1)
        speeds(CX)

    lax.fori_loop(2, CX, speeds, 0)
    lax.fori_loop(3, CX - 1, functools.partial(stresses, 0), 0)
    wait_recv(edge_halo(0))
    wait_recv(density_halo())
    for i in range(2):
        @pl.when(has_left if i == 0 else has_right)
        def _():
            edge_b[i] = COURANT * (1.0 / edge_b[i])
    end_planes(0)
    for x in (1, 2, CX - 1, CX):
        stresses(0, x)
    densify()
    lax.fori_loop(0, 4, first_product, 0)
    edges_out(1)
    start(edge_halo(1))
    for c in loads_w:
        c.wait()
    wait_recv(forward_halo())
    lax.fori_loop(0, 4, later_products, 0)

    def planes(first, stop, body):
        lax.fori_loop(first, stop, body, 0)

    both = [functools.partial(stresses, t, add=True) for t in range(STEPS)]
    wait_recv(edge_halo(1))
    edges_in(1)
    for x in (1, 2, CX - 1, CX):
        speeds(x)
    both[1](1)
    both[1](CX)
    edges_out(2)
    start(edge_halo(2))
    planes(3, CX - 1, speeds)
    low, high = 2 * GROUPS[0][0] + 1, 2 * (GROUPS[0][0] + GROUPS[0][1]) + 1
    planes(low - 2, high + 2, both[1])
    planes(low - 1, high + 1, speeds)

    def to_mate(n):
        pairs = pl.ds(*GROUPS[n])
        return [
            pltpu.make_async_remote_copy(
                src_ref=gs.at[2 * j + 1 - core, :, pairs],
                dst_ref=rb1.at[j, :, pairs],
                send_sem=r1_s.at[n, j],
                recv_sem=r1_r.at[n, j],
                device_id={"shot": mate},
                device_id_type=pl.DeviceIdType.MESH,
            )
            for j in range(2)
        ]

    def to_cross(n):
        pairs = pl.ds(*GROUPS[n])
        return pltpu.make_async_remote_copy(
            src_ref=s2.at[:, pairs],
            dst_ref=rb2.at[:, pairs],
            send_sem=r2_s.at[n],
            recv_sem=r2_r.at[n],
            device_id={"shot": cross},
            device_id_type=pl.DeviceIdType.MESH,
        )

    def pairs_of(n, body):
        first, count = GROUPS[n]
        lax.fori_loop(first, first + count, body, 0)

    def slabs(i, carry):
        for k in range(3):
            for xx in range(2):
                for s in range(4):
                    lo, hi = max(0, 16 * s - 2), min(NY, 16 * s + 18)
                    off = 20 * xx + lo - (16 * s - 2)
                    gs[s, k, i, pl.ds(off, hi - lo), :] = G[k][2 * i + xx, pl.ds(lo, hi - lo), :]
        return carry

    def sum_cross(i, carry):
        for k in range(3):
            s2[k, i] = gs[2 * (1 - chip) + core, k, i] + rb1[1 - chip, k, i]
        return carry

    def pass_on(n):
        for c in to_mate(n):
            c.wait_recv()
        pairs_of(n, sum_cross)
        to_cross(n).start()

    for n, (first, count) in enumerate(GROUPS):
        planes(2 * first + 1, 2 * (first + count) + 1, both[2])
        pairs_of(n, slabs)
        for c in to_mate(n):
            c.start()
        if n == 0:
            planes(2, low - 2, both[1])
            planes(high + 2, CX, both[1])
            pass_on(0)
            planes(2, low - 1, speeds)
            planes(high + 1, CX, speeds)
            wait_recv(edge_halo(2))
            edges_in(2)
            speeds(1)
            speeds(CX)
        elif n > 1:
            pass_on(n - 1)
    pass_on(len(GROUPS) - 1)

    def sum_own(i, carry):
        for k in range(3):
            for xx in range(2):
                part = pl.ds(20 * xx, 20)
                total = (gs[2 * chip + core, k, i, part, :] + rb1[chip, k, i, part, :]) + rb2[k, i, part, :]
                h0[k, 2 + 2 * i + xx, pl.ds(8, 20), :] = total
        return carry

    rim = pl.ds(8, 24)
    grad_halo = (
        [send(h0.at[:, pl.ds(2, 2), rim], h0.at[:, pl.ds(CX + 2, 2), rim], gx_s.at[0], gx_r.at[0], left)],
        [send(h0.at[:, pl.ds(CX, 2), rim], h0.at[:, pl.ds(0, 2), rim], gx_s.at[1], gx_r.at[1], right)],
    )
    for n in range(len(GROUPS)):
        to_cross(n).wait_recv()
        pairs_of(n, sum_own)
        if n == 2:
            start(grad_halo)
    wait_recv(grad_halo)
    wait_send(grad_halo)

    for step in range(STEPS):
        wait_send(edge_halo(step))
    wait_send(density_halo())
    wait_send(forward_halo())

    def channel_sent(k, carry):
        channel_copy(k).wait_send()
        return carry

    lax.fori_loop(1, N_SPACE, channel_sent, 0)
    for n in range(len(GROUPS)):
        for c in to_mate(n):
            c.wait_send()
        to_cross(n).wait_send()


def finish(f0, f1, f2, f3, f4, f5, f6, f7, f8, h0, out_adj, out_grad, h1, og, sem):
    me = lax.axis_index("space")
    sh = lax.axis_index("shot")
    fields = (f0, f1, f2, f3, f4, f5, f6, f7, f8)
    stores = [pltpu.make_async_copy(f.at[pl.ds(1, CX), pl.ds(PAD, NY)], out_adj.at[0, k], sem.at[k]) for k, f in enumerate(fields)]
    for c in stores:
        c.start()

    def near(h, k, p, lo, n):
        def at(dp=0, dy=0):
            return h[k, p + dp, pl.ds(lo + dy, n), :]

        mid = at()
        lane = lane_of(n)
        total = at(1) + at(-1) + at(0, 1) + at(0, -1)
        total = total + jnp.where(lane == NZ - 1, 0.0, pltpu.roll(mid, NZ - 1, 1)) + jnp.where(lane == 0, 0.0, pltpu.roll(mid, 1, 1))
        return mid + KAPPA * (total - 6.0 * mid)

    def sweep_one(p, carry):
        gx = CX * me + p - 2
        gy = 16 * sh - 2 + lax.broadcasted_iota(I32, (24, NZ), 0)
        keep = (gy >= 0) & (gy < NY) & (gx >= 0) & (gx < NX)
        for k in range(3):
            h1[k, p, pl.ds(8, 24), :] = jnp.where(keep, near(h0, k, p, 8, 24), 0.0)
        return carry

    lax.fori_loop(1, CX + 3, sweep_one, 0)

    def sweep_two(x, carry):
        for k in range(3):
            og[k, x] = near(h1, k, x + 2, 10, 16)
        return carry

    lax.fori_loop(0, CX, sweep_two, 0)
    grad_out = pltpu.make_async_copy(og, out_grad, sem.at[9])
    grad_out.start()
    grad_out.wait()
    for c in stores:
        c.wait()


def local(adjoint_state, forward_velocity, vp, shear_ratio, density, residuals, owner, cell):
    res = residuals.reshape(STEPS, 1, CH_DEV)
    own = owner.reshape(1, CH_DEV)
    cells = cell.reshape(1, CH_DEV)
    hbm = pl.BlockSpec(memory_space=pltpu.HBM)
    vmem = pl.BlockSpec(memory_space=pltpu.VMEM)
    volume = pltpu.VMEM((CX, NY, NZ), F32)
    dma = pltpu.SemaphoreType.DMA
    edges = pltpu.VMEM((STEPS, 3, NY, NZ), F32)
    pair = pltpu.VMEM((2, NY, NZ), F32)
    count = len(GROUPS)
    scratch = (
        [
            pltpu.VMEM((STEPS + 1, 3, CX + 2, PY, NZ), F32),
            pltpu.VMEM((STEPS, CX, NY, NZ), F32),
        ]
        + [volume] * 6
        + [edges] * 4
        + [pair] * 2
        + [
            pltpu.VMEM((STEPS, 1, CH_DEV), F32),
            pltpu.VMEM((1, CH_DEV), I32),
            pltpu.VMEM((1, CH_DEV), I32),
            pltpu.VMEM((N_SPACE, 8, CAP), F32),
            pltpu.VMEM((N_SPACE, 8, CAP), F32),
            pltpu.VMEM((N_SPACE, CX * NY, CAP), BF16),
            pltpu.VMEM((STEPS, N_SPACE, 2 * NZ, CAP), BF16),
            pltpu.VMEM((4, 3, CX // 2, 40, NZ), F32),
            pltpu.VMEM((2, 3, CX // 2, 40, NZ), F32),
            pltpu.VMEM((3, CX // 2, 40, NZ), F32),
            pltpu.VMEM((3, CX // 2, 40, NZ), F32),
        ]
        + [dma((9,)), dma((4,)), dma((3,)), dma((10, 2)), dma((3,))]
        + [dma((STEPS, 2)), dma((STEPS, 2)), dma((2,)), dma((2,)), dma((2,)), dma((2,)), dma((N_SPACE,)), dma((N_SPACE,))]
        + [dma((count, 2)), dma((count, 2)), dma((count,)), dma((count,)), dma((2,)), dma((2,))]
    )
    held = [(CX + 2, PY, NZ)] * 9 + [(3, CX + 4, 40, NZ)]
    given = (adjoint_state, forward_velocity, vp, shear_ratio, density, res, own, cells)
    given = [pltpu.with_memory_space_constraint(a, pltpu.HBM) for a in given]
    kept = pl.pallas_call(
        kernel,
        out_shape=tuple(pltpu.VMEM(shape, F32) for shape in held),
        in_specs=[hbm] * 8,
        out_specs=(vmem,) * len(held),
        scratch_shapes=scratch,
        compiler_params=pltpu.CompilerParams(collective_id=0, has_side_effects=True, vmem_limit_bytes=44 * 1024 * 1024),
    )(*given)
    kept = [pltpu.with_memory_space_constraint(a, pltpu.VMEM) for a in kept]
    return pl.pallas_call(
        finish,
        out_shape=(
            jax.ShapeDtypeStruct((1, 9, CX, NY, NZ), F32),
            jax.ShapeDtypeStruct((3, CX, 16, NZ), F32),
        ),
        in_specs=[vmem] * len(held),
        out_specs=(hbm, hbm),
        scratch_shapes=[pltpu.VMEM((3, CX + 4, 40, NZ), F32), pltpu.VMEM((3, CX, 16, NZ), F32), dma((10,))],
        compiler_params=pltpu.CompilerParams(vmem_limit_bytes=8 * 1024 * 1024),
    )(*kept)


def solution(mesh):
    in_specs = (
        P("shot", None, "space", None, None),
        P("shot", None, None, "space", None, None),
        P("space", None, None),
        P("space", None, None),
        P("space", None, None),
        P("shot", None, "space"),
        P("space", None),
        P("space"),
    )
    out_specs = (P("shot", None, "space", None, None), P(None, "space", "shot", None))
    return jax.shard_map(local, mesh=mesh, in_specs=in_specs, out_specs=out_specs, check_vma=False)
```

```python
import functools

import jax
import jax.numpy as jnp
from jax import lax
from jax.experimental import pallas as pl
from jax.experimental.pallas import tpu as pltpu
from jax.sharding import PartitionSpec as P

STEPS = 3
CX, NY, NZ = 16, 64, 128
NX = 512
N_SPACE = 32
CH_DEV = 1024
CAP = 128
COURANT = 0.3
KAPPA = 0.15
ROWS = 32
PAD = 8
PY = NY + 2 * PAD
VX, VY, VZ, SXX, SYY, SZZ, SXY, SXZ, SYZ = range(9)
GROUPS = ((3, 2), (0, 1), (7, 1), (1, 2), (5, 2))
F32, BF16, I32 = jnp.float32, jnp.bfloat16, jnp.int32


def nt(a, b):
    return lax.dot_general(a, b, (((1,), (1,)), ((), ())), preferred_element_type=F32)


def lane_of(rows):
    return lax.broadcasted_iota(I32, (rows, NZ), 1)


def zminus(f):
    rolled = pltpu.roll(f, 1, 1)
    return f - jnp.where(lane_of(f.shape[0]) == 0, 0.0, rolled)


def zplus(f):
    rolled = pltpu.roll(f, NZ - 1, 1)
    return jnp.where(lane_of(f.shape[0]) == NZ - 1, 0.0, rolled) - f


def near(h, k, p, lo, n):
    def at(dp=0, dy=0):
        return h[k, p + dp, pl.ds(lo + dy, n), :]

    mid = at()
    lane = lane_of(n)
    total = at(1) + at(-1) + at(0, 1) + at(0, -1)
    total = total + jnp.where(lane == NZ - 1, 0.0, pltpu.roll(mid, NZ - 1, 1)) + jnp.where(lane == 0, 0.0, pltpu.roll(mid, 1, 1))
    return mid + KAPPA * (total - 6.0 * mid)


def kernel(
    adj, fwd, vp_h, sr_h, dn_h, res_h, own_h, cell_h,
    f0, f1, f2, f3, f4, f5, f6, f7, f8, h1,
    fw, dense, cb, cl, cm, g0, g1, g2,
    to_left, to_right, from_left, from_right, edge_b, rho_end,
    res, own, cell, packed, arrived, a_one, b_one,
    gs, rb1, s2, rb2, h0,
    load_f, load_w, load_p, load_e, load_c,
    halo_s, halo_r, eb_s, eb_r, fh_s, fh_r, a2a_s, a2a_r,
    r1_s, r1_r, r2_s, r2_r, gx_s, gx_r,
):
    F = (f0, f1, f2, f3, f4, f5, f6, f7, f8)
    G = (g0, g1, g2)
    me = lax.axis_index("space")
    sh = lax.axis_index("shot")
    core = sh % 2
    chip = sh // 2
    has_left = me > 0
    has_right = me < N_SPACE - 1
    left = (me + N_SPACE - 1) % N_SPACE
    right = (me + 1) % N_SPACE
    mate = 2 * chip + (1 - core)
    cross = 2 * (1 - chip) + core
    inner = pl.ds(PAD, NY)

    ends = ((0, 0), (1, CX - 1))
    middle = pl.ds(1, CX - 2)
    loads_e = [pltpu.make_async_copy(dn_h.at[x], cb.at[x], load_e.at[9, i]) for i, x in ends]
    loads_e += [pltpu.make_async_copy(adj.at[0, k, x], F[k].at[x + 1, inner], load_e.at[k, i]) for k in range(9) for i, x in ends]
    loads_p = [pltpu.make_async_copy(vp_h, cl, load_p.at[0]), pltpu.make_async_copy(sr_h, cm, load_p.at[1])]
    loads_p.append(pltpu.make_async_copy(dn_h.at[middle], cb.at[middle], load_p.at[2]))
    loads_f = [pltpu.make_async_copy(adj.at[0, k, middle], F[k].at[pl.ds(2, CX - 2), inner], load_f.at[k]) for k in range(9)]
    loads_w = [pltpu.make_async_copy(fwd.at[0, t], fw.at[t, :, pl.ds(1, CX), inner], load_w.at[t]) for t in range(STEPS + 1)]
    loads_c = [pltpu.make_async_copy(src, dst, load_c.at[i]) for i, (src, dst) in enumerate(((own_h, own), (cell_h, cell), (res_h, res)))]
    for c in loads_e + loads_c + loads_f + loads_p + loads_w:
        c.start()

    barrier = pltpu.get_barrier_semaphore()

    def greet(k, carry):
        pl.semaphore_signal(barrier, inc=1, device_id={"space": (me + k) % N_SPACE}, device_id_type=pl.DeviceIdType.MESH)
        return carry

    for other in (mate, cross):
        pl.semaphore_signal(barrier, inc=1, device_id={"shot": other}, device_id_type=pl.DeviceIdType.MESH)
    lax.fori_loop(1, N_SPACE, greet, 0)

    zpad = jnp.zeros((PAD, NZ), F32)

    def zero_pads(x, carry):
        for k in (VX, VY, VZ, SYY, SXY, SYZ):
            F[k][x, pl.ds(0, PAD), :] = zpad
            F[k][x, pl.ds(PAD + NY, PAD), :] = zpad
        for t in range(STEPS):
            for k in range(3):
                fw[t, k, x, pl.ds(0, PAD), :] = zpad
                fw[t, k, x, pl.ds(PAD + NY, PAD), :] = zpad
        return carry

    zero_pads(1, 0)
    zero_pads(CX, 0)
    zplane = jnp.zeros((NY, NZ), F32)

    @pl.when(me == 0)
    def _():
        edge_b[0] = zplane
        for t in range(STEPS):
            fw[t, 0, 0, inner, :] = zplane
            for k in range(3):
                from_left[t, k] = zplane

    @pl.when(me == N_SPACE - 1)
    def _():
        edge_b[1] = zplane
        for t in range(STEPS):
            for k in range(3):
                from_right[t, k] = zplane
            for k in (1, 2):
                fw[t, k, CX + 1, inner, :] = zplane

    def edges_out(step):
        for y in range(0, NY, ROWS):
            def at(k, x, dy=0):
                return F[k][x, pl.ds(PAD + y + dy, ROWS), :]

            rows = pl.ds(y, ROWS)
            b = cb[0, rows, :]
            syz = at(SYZ, 1)
            to_left[step, 0, rows, :] = at(SXX, 1)
            to_left[step, 1, rows, :] = at(VY, 1) + b * (at(SXY, 1) + (at(SYY, 1, 1) - at(SYY, 1)) + zminus(syz))
            to_left[step, 2, rows, :] = at(VZ, 1) + b * (at(SXZ, 1) + (syz - at(SYZ, 1, -1)) + zplus(at(SZZ, 1)))
            b = cb[CX - 1, rows, :]
            sxy, sxz = at(SXY, CX), at(SXZ, CX)
            to_right[step, 0, rows, :] = at(VX, CX) + b * ((sxy - at(SXY, CX, -1)) + zminus(sxz) - at(SXX, CX))
            to_right[step, 1, rows, :] = sxy
            to_right[step, 2, rows, :] = sxz

    def edges_in(step):
        for y in range(0, NY, ROWS):
            rows = pl.ds(y, ROWS)
            here = pl.ds(PAD + y, ROWS)
            b = edge_b[0, rows, :]
            F[VX][0, here, :] = from_left[step, 0, rows, :] + b * F[SXX][1, here, :]
            F[SXY][0, here, :] = from_left[step, 1, rows, :]
            F[SXZ][0, here, :] = from_left[step, 2, rows, :]
            b = edge_b[1, rows, :]
            F[SXX][CX + 1, here, :] = from_right[step, 0, rows, :]
            F[VY][CX + 1, here, :] = from_right[step, 1, rows, :] - b * F[SXY][CX, here, :]
            F[VZ][CX + 1, here, :] = from_right[step, 2, rows, :] - b * F[SXZ][CX, here, :]

    for c in loads_e:
        c.wait()
    for i, x in ends:
        rho = cb[x]
        rho_end[i] = rho
        cb[x] = COURANT * (1.0 / rho)
    edges_out(0)

    pl.semaphore_wait(barrier, N_SPACE + 1)

    def send(src, dst, s, r, to):
        return pltpu.make_async_remote_copy(
            src_ref=src, dst_ref=dst, send_sem=s, recv_sem=r, device_id={"space": to}, device_id_type=pl.DeviceIdType.MESH
        )

    def edge_halo(step):
        return (
            [send(to_left.at[step], from_right.at[step], halo_s.at[step, 0], halo_r.at[step, 0], left)],
            [send(to_right.at[step], from_left.at[step], halo_s.at[step, 1], halo_r.at[step, 1], right)],
        )

    def density_halo():
        return (
            [send(dn_h.at[0], edge_b.at[1], eb_s.at[0], eb_r.at[0], left)],
            [send(dn_h.at[CX - 1], edge_b.at[0], eb_s.at[1], eb_r.at[1], right)],
        )

    def forward_halo():
        return (
            [send(fwd.at[0, pl.ds(0, STEPS), pl.ds(1, 2), 0], fw.at[pl.ds(0, STEPS), pl.ds(1, 2), CX + 1, inner], fh_s.at[0], fh_r.at[0], left)],
            [send(fwd.at[0, pl.ds(0, STEPS), 0, CX - 1], fw.at[pl.ds(0, STEPS), 0, 0, inner], fh_s.at[1], fh_r.at[1], right)],
        )

    def start(pair):
        @pl.when(has_left)
        def _():
            for c in pair[0]:
                c.start()

        @pl.when(has_right)
        def _():
            for c in pair[1]:
                c.start()

    def wait_recv(pair):
        @pl.when(has_right)
        def _():
            for c in pair[0]:
                c.wait_recv()

        @pl.when(has_left)
        def _():
            for c in pair[1]:
                c.wait_recv()

    def wait_send(pair):
        @pl.when(has_left)
        def _():
            for c in pair[0]:
                c.wait_send()

        @pl.when(has_right)
        def _():
            for c in pair[1]:
                c.wait_send()

    start(edge_halo(0))
    start(density_halo())

    for c in loads_c:
        c.wait()
    blk = 256
    upper = (lax.broadcasted_iota(I32, (blk, blk), 0) < lax.broadcasted_iota(I32, (blk, blk), 1)).astype(F32).astype(BF16)
    carry_n = jnp.zeros((N_SPACE, 1), F32)
    acc = jnp.zeros((N_SPACE * 16, CAP), F32)
    for b in range(CH_DEV // blk):
        lanes = pl.ds(b * blk, blk)
        o = own[:, lanes]
        oh = (o == lax.broadcasted_iota(I32, (N_SPACE, blk), 0)).astype(F32)
        ranks = jnp.dot(oh.astype(BF16), upper, preferred_element_type=F32) + carry_n
        carry_n = carry_n + jnp.sum(oh, axis=1, keepdims=True)
        rank = jnp.sum(oh * ranks, axis=0, keepdims=True)
        slot = (rank.astype(I32) == lax.broadcasted_iota(I32, (CAP, blk), 0)).astype(F32).astype(BF16)
        cl_ = cell[:, lanes]
        r = [res[t, :, lanes] for t in range(STEPS)]
        hi = [v.astype(BF16).astype(F32) for v in r]
        zero = jnp.zeros((1, blk), F32)
        rows = (
            hi
            + [(cl_ >> 13).astype(F32), ((cl_ >> 7) & 63).astype(F32), (cl_ & 127).astype(F32), zero, zero]
            + [a - h for a, h in zip(r, hi)]
            + [zero] * 5
        )
        payload = jnp.concatenate(rows, axis=0)
        lhs = (oh[:, None, :] * payload[None, :, :]).reshape(N_SPACE * 16, blk).astype(BF16)
        acc = acc + nt(lhs, slot)
    acc = acc.reshape(N_SPACE, 16, CAP)
    packed[...] = acc[:, :8, :] + acc[:, 8:, :]

    def channel_copy(k):
        to = (me + k) % N_SPACE
        return send(packed.at[to], arrived.at[me], a2a_s.at[k], a2a_r.at[k], to)

    def channel_start(k, carry):
        channel_copy(k).start()
        return carry

    lax.fori_loop(1, N_SPACE, channel_start, 0)
    start(forward_halo())
    arrived[me] = packed[me]

    lax.fori_loop(2, CX, zero_pads, 0)

    def zero_h(x, carry):
        for k in range(3):
            h0[k, x, :, :] = jnp.zeros((40, NZ), F32)
        return carry

    lax.fori_loop(0, CX + 4, zero_h, 0)

    def zero_gs(i, carry):
        for k in range(3):
            for xx in range(2):
                gs[0, k, i, pl.ds(20 * xx, 2), :] = jnp.zeros((2, NZ), F32)
                gs[3, k, i, pl.ds(20 * xx + 18, 2), :] = jnp.zeros((2, NZ), F32)
        return carry

    lax.fori_loop(0, CX // 2, zero_gs, 0)

    for c in loads_p:
        c.wait()

    def lame(x, rho):
        vp, ratio = cl[x], cm[x]
        vs = ratio * vp
        mu = rho * vs * vs
        cl[x] = COURANT * (rho * vp * vp - 2.0 * mu)
        cm[x] = COURANT * mu

    def params(x, carry):
        rho = cb[x]
        cb[x] = COURANT * (1.0 / rho)
        lame(x, rho)
        return carry

    lax.fori_loop(1, CX - 1, params, 0)
    for i, x in ends:
        lame(x, rho_end[i])
    for c in loads_f:
        c.wait()

    def speeds(x, carry=0):
        for y in range(0, NY, ROWS):
            def at(k, dx=0, dy=0):
                return F[k][x + dx, pl.ds(PAD + y + dy, ROWS), :]

            here = pl.ds(PAD + y, ROWS)
            b = cb[x - 1, pl.ds(y, ROWS), :]
            sxy, sxz, syz = at(SXY), at(SXZ), at(SYZ)
            vx = at(VX) + b * ((at(SXX, 1) - at(SXX)) + (sxy - at(SXY, 0, -1)) + zminus(sxz))
            vy = at(VY) + b * ((sxy - at(SXY, -1)) + (at(SYY, 0, 1) - at(SYY)) + zminus(syz))
            vz = at(VZ) + b * ((sxz - at(SXZ, -1)) + (syz - at(SYZ, 0, -1)) + zplus(at(SZZ)))
            F[VX][x, here, :] = vx
            F[VY][x, here, :] = vy
            F[VZ][x, here, :] = vz
        return carry

    def stresses(step, x, carry=0, add=False):
        for y in range(0, NY, ROWS):
            def at(k, dx=0, dy=0):
                return F[k][x + dx, pl.ds(PAD + y + dy, ROWS), :]

            here = pl.ds(PAD + y, ROWS)
            flat = pl.ds(y, ROWS)
            lam, mu = cl[x - 1, flat, :], cm[x - 1, flat, :]
            vx, vy, vz = at(VX), at(VY), at(VZ)
            exx = vx - at(VX, -1)
            eyy = vy - at(VY, 0, -1)
            ezz = zminus(vz)
            base = lam * (exx + eyy + ezz)
            mu2 = mu + mu
            szz = at(SZZ) + (base + mu2 * ezz)
            new = [
                at(SXX) + (base + mu2 * exx),
                at(SYY) + (base + mu2 * eyy),
                szz + dense[step, x - 1, flat, :] if step > 0 else szz,
                at(SXY) + mu * ((at(VY, 1) - vy) + (at(VX, 0, 1) - vx)),
                at(SXZ) + mu * ((at(VZ, 1) - vz) + zplus(vx)),
                at(SYZ) + mu * ((at(VZ, 0, 1) - vz) + zplus(vy)),
            ]
            for k, v in zip((SXX, SYY, SZZ, SXY, SXZ, SYZ), new):
                F[k][x, here, :] = v
            if add:
                add_terms(step, x, y, vx, vy, vz, *new)
        return carry

    def add_terms(step, x, y, vx, vy, vz, sxx, syy, szz, sxy, sxz, syz):
        def u(k, dx=0, dy=0):
            return fw[step, k, x + dx, pl.ds(PAD + y + dy, ROWS), :]

        def w(k):
            return fw[step + 1, k, x, pl.ds(PAD + y, ROWS), :]

        flat = pl.ds(y, ROWS)
        ux, uy, uz = u(0), u(1), u(2)
        fxx = ux - u(0, -1)
        fyy = uy - u(1, 0, -1)
        fzz = zminus(uz)
        lam = (fxx + fyy + fzz) * (sxx + syy + szz)
        mu = (
            2.0 * (fxx * sxx + fyy * syy + fzz * szz)
            + ((u(1, 1) - uy) + (u(0, 0, 1) - ux)) * sxy
            + ((u(2, 1) - uz) + zplus(ux)) * sxz
            + ((u(2, 0, 1) - uz) + zplus(uy)) * syz
        )
        rho = vx * (w(0) - ux) + vy * (w(1) - uy) + vz * (w(2) - uz)
        for ref, term in zip(G, (lam, mu, rho)):
            ref[x - 1, flat, :] = term if step == 0 else ref[x - 1, flat, :] + term

    def gradients(step, x, carry=0):
        for y in range(0, NY, ROWS):
            add_terms(step, x, y, *[F[k][x, pl.ds(PAD + y, ROWS), :] for k in range(9)])
        return carry

    def tile(v):
        return jnp.broadcast_to(v, (16, CAP)).astype(BF16)

    def values(s, steps):
        row = arrived[s]
        zone = (row[5:6].astype(I32) == lax.broadcasted_iota(I32, (NZ, CAP), 0)).astype(F32).astype(BF16)
        zone = zone.reshape(NZ // 16, 16, CAP)
        for t in steps:
            v = row[t : t + 1]
            hi = v.astype(BF16).astype(F32)
            b_one[t, s, pl.ds(0, NZ), :] = (zone * tile(hi)[None]).reshape(NZ, CAP)
            b_one[t, s, pl.ds(NZ, NZ), :] = (zone * tile(v - hi)[None]).reshape(NZ, CAP)

    def densify():
        def channel_wait(k, carry):
            channel_copy(k).wait_recv()
            return carry

        lax.fori_loop(1, N_SPACE, channel_wait, 0)

        def one_hot(s, carry):
            row = arrived[s]
            x, y = row[3:4].astype(I32), row[4:5].astype(I32)
            yone = (y == lax.broadcasted_iota(I32, (NY, CAP), 0)).astype(F32).astype(BF16)
            yone = yone.reshape(NY // 16, 16, CAP)
            for i in range(CX):
                xone = tile((x == i).astype(F32))
                a_one[s, pl.ds(i * NY, NY), :] = (yone * xone[None]).reshape(NY, CAP)
            values(s, (0,))
            return carry

        lax.fori_loop(0, N_SPACE, one_hot, 0)

    def product(m, t):
        rows = pl.ds(pl.multiple_of(m * 256, 256), 256)
        got = nt(
            jnp.concatenate([a_one[s, rows, :] for s in range(N_SPACE)], axis=1),
            jnp.concatenate([b_one[t, s] for s in range(N_SPACE)], axis=1),
        )
        dense[t, pl.ds(4 * m, 4), :, :] = (got[:, :NZ] + got[:, NZ:]).reshape(4, NY, NZ)

    def first_product(m, carry):
        for i in range(N_SPACE // 4):
            values(N_SPACE // 4 * m + i, (1, 2))
        product(m, 0)
        for i in range(4):
            x = 4 * m + i + 1
            F[SZZ][x, inner, :] = F[SZZ][x, inner, :] + dense[0, x - 1]
        return carry

    def later_products(m, carry):
        for t in range(1, STEPS):
            product(m, t)
        for i in range(4):
            gradients(0, 4 * m + i + 1)
        for i in range(3):
            speeds(3 * m + i + 2)
        return carry

    def end_planes(step):
        edges_in(step)
        speeds(1)
        speeds(CX)

    lax.fori_loop(2, CX, speeds, 0)
    lax.fori_loop(3, CX - 1, functools.partial(stresses, 0), 0)
    wait_recv(edge_halo(0))
    wait_recv(density_halo())
    for i in range(2):
        @pl.when(has_left if i == 0 else has_right)
        def _():
            edge_b[i] = COURANT * (1.0 / edge_b[i])
    end_planes(0)
    for x in (1, 2, CX - 1, CX):
        stresses(0, x)
    densify()
    lax.fori_loop(0, 4, first_product, 0)
    edges_out(1)
    start(edge_halo(1))
    for c in loads_w:
        c.wait()
    wait_recv(forward_halo())
    lax.fori_loop(0, 4, later_products, 0)

    def planes(first, stop, body):
        lax.fori_loop(first, stop, body, 0)

    both = [functools.partial(stresses, t, add=True) for t in range(STEPS)]
    wait_recv(edge_halo(1))
    edges_in(1)
    for x in (1, CX - 2, CX - 1, CX):
        speeds(x)
    both[1](1)
    both[1](CX)
    edges_out(2)
    start(edge_halo(2))
    low, high = 2 * GROUPS[0][0] + 1, 2 * (GROUPS[0][0] + GROUPS[0][1]) + 1
    planes(low - 2, high + 2, both[1])
    planes(low - 1, high + 1, speeds)

    def to_mate(n):
        pairs = pl.ds(*GROUPS[n])
        return [
            pltpu.make_async_remote_copy(
                src_ref=gs.at[2 * j + 1 - core, :, pairs],
                dst_ref=rb1.at[j, :, pairs],
                send_sem=r1_s.at[n, j],
                recv_sem=r1_r.at[n, j],
                device_id={"shot": mate},
                device_id_type=pl.DeviceIdType.MESH,
            )
            for j in range(2)
        ]

    def to_cross(n):
        pairs = pl.ds(*GROUPS[n])
        return pltpu.make_async_remote_copy(
            src_ref=s2.at[:, pairs],
            dst_ref=rb2.at[:, pairs],
            send_sem=r2_s.at[n],
            recv_sem=r2_r.at[n],
            device_id={"shot": cross},
            device_id_type=pl.DeviceIdType.MESH,
        )

    def pairs_of(n, body):
        first, count = GROUPS[n]
        lax.fori_loop(first, first + count, body, 0)

    def slabs(i, carry):
        for k in range(3):
            for xx in range(2):
                for s in range(4):
                    lo, hi = max(0, 16 * s - 2), min(NY, 16 * s + 18)
                    off = 20 * xx + lo - (16 * s - 2)
                    gs[s, k, i, pl.ds(off, hi - lo), :] = G[k][2 * i + xx, pl.ds(lo, hi - lo), :]
        return carry

    def sum_cross(i, carry):
        for k in range(3):
            s2[k, i] = gs[2 * (1 - chip) + core, k, i] + rb1[1 - chip, k, i]
        return carry

    def pass_on(n):
        for c in to_mate(n):
            c.wait_recv()
        pairs_of(n, sum_cross)
        to_cross(n).start()

    for n, (first, count) in enumerate(GROUPS):
        planes(2 * first + 1, 2 * (first + count) + 1, both[2])
        pairs_of(n, slabs)
        for c in to_mate(n):
            c.start()
        if n == 0:
            planes(2, low - 2, both[1])
            planes(high + 2, CX, both[1])
            pass_on(0)
            planes(2, low - 1, speeds)
            planes(high + 1, CX, speeds)
            wait_recv(edge_halo(2))
            edges_in(2)
            speeds(1)
            speeds(CX)
        elif n > 1:
            pass_on(n - 1)
    pass_on(len(GROUPS) - 1)

    def sum_own(i, carry):
        for k in range(3):
            for xx in range(2):
                part = pl.ds(20 * xx, 20)
                total = (gs[2 * chip + core, k, i, part, :] + rb1[chip, k, i, part, :]) + rb2[k, i, part, :]
                h0[k, 2 + 2 * i + xx, pl.ds(8, 20), :] = total
        return carry

    rim = pl.ds(8, 24)
    grad_halo = (
        [send(h0.at[:, pl.ds(2, 2), rim], h0.at[:, pl.ds(CX + 2, 2), rim], gx_s.at[0], gx_r.at[0], left)],
        [send(h0.at[:, pl.ds(CX, 2), rim], h0.at[:, pl.ds(0, 2), rim], gx_s.at[1], gx_r.at[1], right)],
    )
    def sweep_one(p, carry):
        gx = CX * me + p - 2
        gy = 16 * sh - 2 + lax.broadcasted_iota(I32, (24, NZ), 0)
        keep = (gy >= 0) & (gy < NY) & (gx >= 0) & (gx < NX)
        for k in range(3):
            h1[k, p, rim, :] = jnp.where(keep, near(h0, k, p, 8, 24), 0.0)
        return carry

    for n in range(len(GROUPS)):
        to_cross(n).wait_recv()
        pairs_of(n, sum_own)
        if n == 2:
            start(grad_halo)
        if n == 3:
            planes(3, 11, sweep_one)
        if n == 4:
            planes(11, CX + 1, sweep_one)
    wait_recv(grad_halo)
    planes(1, 3, sweep_one)
    planes(CX + 1, CX + 3, sweep_one)
    wait_send(grad_halo)

    for step in range(STEPS):
        wait_send(edge_halo(step))
    wait_send(density_halo())
    wait_send(forward_halo())

    def channel_sent(k, carry):
        channel_copy(k).wait_send()
        return carry

    lax.fori_loop(1, N_SPACE, channel_sent, 0)
    for n in range(len(GROUPS)):
        for c in to_mate(n):
            c.wait_send()
        to_cross(n).wait_send()


def finish(f0, f1, f2, f3, f4, f5, f6, f7, f8, h1, out_adj, out_grad, og, sem):
    fields = (f0, f1, f2, f3, f4, f5, f6, f7, f8)
    stores = [pltpu.make_async_copy(f.at[pl.ds(1, CX), pl.ds(PAD, NY)], out_adj.at[0, k], sem.at[k]) for k, f in enumerate(fields)]
    for c in stores:
        c.start()

    def sweep_two(x, carry):
        for k in range(3):
            og[k, x] = near(h1, k, x + 2, 10, 16)
        return carry

    half = CX // 2
    parts = []
    for i in range(2):
        lax.fori_loop(half * i, half * (i + 1), sweep_two, 0)
        part = pl.ds(half * i, half)
        parts.append(pltpu.make_async_copy(og.at[:, part], out_grad.at[:, part], sem.at[9 + i]))
        parts[i].start()
    for c in parts:
        c.wait()
    for c in stores:
        c.wait()


def local(adjoint_state, forward_velocity, vp, shear_ratio, density, residuals, owner, cell):
    res = residuals.reshape(STEPS, 1, CH_DEV)
    own = owner.reshape(1, CH_DEV)
    cells = cell.reshape(1, CH_DEV)
    hbm = pl.BlockSpec(memory_space=pltpu.HBM)
    vmem = pl.BlockSpec(memory_space=pltpu.VMEM)
    volume = pltpu.VMEM((CX, NY, NZ), F32)
    dma = pltpu.SemaphoreType.DMA
    edges = pltpu.VMEM((STEPS, 3, NY, NZ), F32)
    pair = pltpu.VMEM((2, NY, NZ), F32)
    count = len(GROUPS)
    scratch = (
        [
            pltpu.VMEM((STEPS + 1, 3, CX + 2, PY, NZ), F32),
            pltpu.VMEM((STEPS, CX, NY, NZ), F32),
        ]
        + [volume] * 6
        + [edges] * 4
        + [pair] * 2
        + [
            pltpu.VMEM((STEPS, 1, CH_DEV), F32),
            pltpu.VMEM((1, CH_DEV), I32),
            pltpu.VMEM((1, CH_DEV), I32),
            pltpu.VMEM((N_SPACE, 8, CAP), F32),
            pltpu.VMEM((N_SPACE, 8, CAP), F32),
            pltpu.VMEM((N_SPACE, CX * NY, CAP), BF16),
            pltpu.VMEM((STEPS, N_SPACE, 2 * NZ, CAP), BF16),
            pltpu.VMEM((4, 3, CX // 2, 40, NZ), F32),
            pltpu.VMEM((2, 3, CX // 2, 40, NZ), F32),
            pltpu.VMEM((3, CX // 2, 40, NZ), F32),
            pltpu.VMEM((3, CX // 2, 40, NZ), F32),
            pltpu.VMEM((3, CX + 4, 40, NZ), F32),
        ]
        + [dma((9,)), dma((4,)), dma((3,)), dma((10, 2)), dma((3,))]
        + [dma((STEPS, 2)), dma((STEPS, 2)), dma((2,)), dma((2,)), dma((2,)), dma((2,)), dma((N_SPACE,)), dma((N_SPACE,))]
        + [dma((count, 2)), dma((count, 2)), dma((count,)), dma((count,)), dma((2,)), dma((2,))]
    )
    held = [(CX + 2, PY, NZ)] * 9 + [(3, CX + 4, 40, NZ)]
    given = (adjoint_state, forward_velocity, vp, shear_ratio, density, res, own, cells)
    given = [pltpu.with_memory_space_constraint(a, pltpu.HBM) for a in given]
    kept = pl.pallas_call(
        kernel,
        out_shape=tuple(pltpu.VMEM(shape, F32) for shape in held),
        in_specs=[hbm] * 8,
        out_specs=(vmem,) * len(held),
        scratch_shapes=scratch,
        compiler_params=pltpu.CompilerParams(collective_id=0, has_side_effects=True, vmem_limit_bytes=44 * 1024 * 1024),
    )(*given)
    kept = [pltpu.with_memory_space_constraint(a, pltpu.VMEM) for a in kept]
    return pl.pallas_call(
        finish,
        out_shape=(
            jax.ShapeDtypeStruct((1, 9, CX, NY, NZ), F32),
            jax.ShapeDtypeStruct((3, CX, 16, NZ), F32),
        ),
        in_specs=[vmem] * len(held),
        out_specs=(hbm, hbm),
        scratch_shapes=[pltpu.VMEM((3, CX, 16, NZ), F32), dma((11,))],
        compiler_params=pltpu.CompilerParams(vmem_limit_bytes=8 * 1024 * 1024),
    )(*kept)


def solution(mesh):
    in_specs = (
        P("shot", None, "space", None, None),
        P("shot", None, None, "space", None, None),
        P("space", None, None),
        P("space", None, None),
        P("space", None, None),
        P("shot", None, "space"),
        P("space", None),
        P("space"),
    )
    out_specs = (P("shot", None, "space", None, None), P(None, "space", "shot", None))
    return jax.shard_map(local, mesh=mesh, in_specs=in_specs, out_specs=out_specs, check_vma=False)
```

```python
import functools

import jax
import jax.numpy as jnp
from jax import lax
from jax.experimental import pallas as pl
from jax.experimental.pallas import tpu as pltpu
from jax.sharding import PartitionSpec as P

STEPS = 3
CX, NY, NZ = 16, 64, 128
NX = 512
N_SPACE = 32
CH_DEV = 1024
CAP = 128
COURANT = 0.3
KAPPA = 0.15
ROWS = 32
PAD = 8
PY = NY + 2 * PAD
VX, VY, VZ, SXX, SYY, SZZ, SXY, SXZ, SYZ = range(9)
GROUPS = ((3, 2), (0, 1), (7, 1), (1, 2), (5, 2))
F32, BF16, I32 = jnp.float32, jnp.bfloat16, jnp.int32


def nt(a, b):
    return lax.dot_general(a, b, (((1,), (1,)), ((), ())), preferred_element_type=F32)


def lane_of(rows):
    return lax.broadcasted_iota(I32, (rows, NZ), 1)


def zminus(f):
    rolled = pltpu.roll(f, 1, 1)
    return f - jnp.where(lane_of(f.shape[0]) == 0, 0.0, rolled)


def zplus(f):
    rolled = pltpu.roll(f, NZ - 1, 1)
    return jnp.where(lane_of(f.shape[0]) == NZ - 1, 0.0, rolled) - f


def near(h, k, p, lo, n):
    def at(dp=0, dy=0):
        return h[k, p + dp, pl.ds(lo + dy, n), :]

    mid = at()
    lane = lane_of(n)
    total = at(1) + at(-1) + at(0, 1) + at(0, -1)
    total = total + jnp.where(lane == NZ - 1, 0.0, pltpu.roll(mid, NZ - 1, 1)) + jnp.where(lane == 0, 0.0, pltpu.roll(mid, 1, 1))
    return mid + KAPPA * (total - 6.0 * mid)


def kernel(
    adj, fwd, vp_h, sr_h, dn_h, res_h, own_h, cell_h,
    f0, f1, f2, f3, f4, f5, f6, f7, f8, h1,
    fw, dense, cb, cl, cm, g0, g1, g2,
    to_left, to_right, from_left, from_right, edge_b, rho_end,
    res, own, cell, packed, arrived, a_one, b_one,
    gs, rb1, s2, rb2, h0,
    load_f, load_w, load_p, load_e, load_c,
    halo_s, halo_r, eb_s, eb_r, fh_s, fh_r, a2a_s, a2a_r,
    r1_s, r1_r, r2_s, r2_r, gx_s, gx_r,
):
    F = (f0, f1, f2, f3, f4, f5, f6, f7, f8)
    G = (g0, g1, g2)
    me = lax.axis_index("space")
    sh = lax.axis_index("shot")
    core = sh % 2
    chip = sh // 2
    has_left = me > 0
    has_right = me < N_SPACE - 1
    left = (me + N_SPACE - 1) % N_SPACE
    right = (me + 1) % N_SPACE
    mate = 2 * chip + (1 - core)
    cross = 2 * (1 - chip) + core
    inner = pl.ds(PAD, NY)

    ends = ((0, 0), (1, CX - 1))
    middle = pl.ds(1, CX - 2)
    loads_e = [pltpu.make_async_copy(dn_h.at[x], cb.at[x], load_e.at[9, i]) for i, x in ends]
    loads_e += [pltpu.make_async_copy(adj.at[0, k, x], F[k].at[x + 1, inner], load_e.at[k, i]) for k in range(9) for i, x in ends]
    loads_p = [pltpu.make_async_copy(vp_h, cl, load_p.at[0]), pltpu.make_async_copy(sr_h, cm, load_p.at[1])]
    loads_p.append(pltpu.make_async_copy(dn_h.at[middle], cb.at[middle], load_p.at[2]))
    loads_f = [pltpu.make_async_copy(adj.at[0, k, middle], F[k].at[pl.ds(2, CX - 2), inner], load_f.at[k]) for k in range(9)]
    loads_w = [pltpu.make_async_copy(fwd.at[0, t], fw.at[t, :, pl.ds(1, CX), inner], load_w.at[t]) for t in range(STEPS + 1)]
    loads_c = [pltpu.make_async_copy(src, dst, load_c.at[i]) for i, (src, dst) in enumerate(((own_h, own), (cell_h, cell), (res_h, res)))]
    for c in loads_e + loads_c + loads_f + loads_p + loads_w:
        c.start()

    barrier = pltpu.get_barrier_semaphore()

    def greet(k, carry):
        pl.semaphore_signal(barrier, inc=1, device_id={"space": (me + k) % N_SPACE}, device_id_type=pl.DeviceIdType.MESH)
        return carry

    for other in (mate, cross):
        pl.semaphore_signal(barrier, inc=1, device_id={"shot": other}, device_id_type=pl.DeviceIdType.MESH)
    lax.fori_loop(1, N_SPACE, greet, 0)

    zpad = jnp.zeros((PAD, NZ), F32)

    def zero_pads(x, carry):
        for k in (VX, VY, VZ, SYY, SXY, SYZ):
            F[k][x, pl.ds(0, PAD), :] = zpad
            F[k][x, pl.ds(PAD + NY, PAD), :] = zpad
        for t in range(STEPS):
            for k in range(3):
                fw[t, k, x, pl.ds(0, PAD), :] = zpad
                fw[t, k, x, pl.ds(PAD + NY, PAD), :] = zpad
        return carry

    zero_pads(1, 0)
    zero_pads(CX, 0)
    zplane = jnp.zeros((NY, NZ), F32)

    @pl.when(me == 0)
    def _():
        edge_b[0] = zplane
        for t in range(STEPS):
            fw[t, 0, 0, inner, :] = zplane
            for k in range(3):
                from_left[t, k] = zplane

    @pl.when(me == N_SPACE - 1)
    def _():
        edge_b[1] = zplane
        for t in range(STEPS):
            for k in range(3):
                from_right[t, k] = zplane
            for k in (1, 2):
                fw[t, k, CX + 1, inner, :] = zplane

    def edges_out(step):
        for y in range(0, NY, ROWS):
            def at(k, x, dy=0):
                return F[k][x, pl.ds(PAD + y + dy, ROWS), :]

            rows = pl.ds(y, ROWS)
            b = cb[0, rows, :]
            syz = at(SYZ, 1)
            to_left[step, 0, rows, :] = at(SXX, 1)
            to_left[step, 1, rows, :] = at(VY, 1) + b * (at(SXY, 1) + (at(SYY, 1, 1) - at(SYY, 1)) + zminus(syz))
            to_left[step, 2, rows, :] = at(VZ, 1) + b * (at(SXZ, 1) + (syz - at(SYZ, 1, -1)) + zplus(at(SZZ, 1)))
            b = cb[CX - 1, rows, :]
            sxy, sxz = at(SXY, CX), at(SXZ, CX)
            to_right[step, 0, rows, :] = at(VX, CX) + b * ((sxy - at(SXY, CX, -1)) + zminus(sxz) - at(SXX, CX))
            to_right[step, 1, rows, :] = sxy
            to_right[step, 2, rows, :] = sxz

    def edges_in(step):
        for y in range(0, NY, ROWS):
            rows = pl.ds(y, ROWS)
            here = pl.ds(PAD + y, ROWS)
            b = edge_b[0, rows, :]
            F[VX][0, here, :] = from_left[step, 0, rows, :] + b * F[SXX][1, here, :]
            F[SXY][0, here, :] = from_left[step, 1, rows, :]
            F[SXZ][0, here, :] = from_left[step, 2, rows, :]
            b = edge_b[1, rows, :]
            F[SXX][CX + 1, here, :] = from_right[step, 0, rows, :]
            F[VY][CX + 1, here, :] = from_right[step, 1, rows, :] - b * F[SXY][CX, here, :]
            F[VZ][CX + 1, here, :] = from_right[step, 2, rows, :] - b * F[SXZ][CX, here, :]

    for c in loads_e:
        c.wait()
    for i, x in ends:
        rho = cb[x]
        rho_end[i] = rho
        cb[x] = COURANT * (1.0 / rho)
    edges_out(0)

    pl.semaphore_wait(barrier, N_SPACE + 1)

    def send(src, dst, s, r, to):
        return pltpu.make_async_remote_copy(
            src_ref=src, dst_ref=dst, send_sem=s, recv_sem=r, device_id={"space": to}, device_id_type=pl.DeviceIdType.MESH
        )

    def edge_halo(step):
        return (
            [send(to_left.at[step], from_right.at[step], halo_s.at[step, 0], halo_r.at[step, 0], left)],
            [send(to_right.at[step], from_left.at[step], halo_s.at[step, 1], halo_r.at[step, 1], right)],
        )

    def density_halo():
        return (
            [send(dn_h.at[0], edge_b.at[1], eb_s.at[0], eb_r.at[0], left)],
            [send(dn_h.at[CX - 1], edge_b.at[0], eb_s.at[1], eb_r.at[1], right)],
        )

    def forward_halo():
        return (
            [send(fwd.at[0, pl.ds(0, STEPS), pl.ds(1, 2), 0], fw.at[pl.ds(0, STEPS), pl.ds(1, 2), CX + 1, inner], fh_s.at[0], fh_r.at[0], left)],
            [send(fwd.at[0, pl.ds(0, STEPS), 0, CX - 1], fw.at[pl.ds(0, STEPS), 0, 0, inner], fh_s.at[1], fh_r.at[1], right)],
        )

    def start(pair):
        @pl.when(has_left)
        def _():
            for c in pair[0]:
                c.start()

        @pl.when(has_right)
        def _():
            for c in pair[1]:
                c.start()

    def wait_recv(pair):
        @pl.when(has_right)
        def _():
            for c in pair[0]:
                c.wait_recv()

        @pl.when(has_left)
        def _():
            for c in pair[1]:
                c.wait_recv()

    def wait_send(pair):
        @pl.when(has_left)
        def _():
            for c in pair[0]:
                c.wait_send()

        @pl.when(has_right)
        def _():
            for c in pair[1]:
                c.wait_send()

    start(edge_halo(0))
    start(density_halo())

    for c in loads_c:
        c.wait()
    blk = 256
    upper = (lax.broadcasted_iota(I32, (blk, blk), 0) < lax.broadcasted_iota(I32, (blk, blk), 1)).astype(F32).astype(BF16)
    carry_n = jnp.zeros((N_SPACE, 1), F32)
    acc = jnp.zeros((N_SPACE * 16, CAP), F32)
    for b in range(CH_DEV // blk):
        lanes = pl.ds(b * blk, blk)
        o = own[:, lanes]
        oh = (o == lax.broadcasted_iota(I32, (N_SPACE, blk), 0)).astype(F32)
        ranks = jnp.dot(oh.astype(BF16), upper, preferred_element_type=F32) + carry_n
        carry_n = carry_n + jnp.sum(oh, axis=1, keepdims=True)
        rank = jnp.sum(oh * ranks, axis=0, keepdims=True)
        slot = (rank.astype(I32) == lax.broadcasted_iota(I32, (CAP, blk), 0)).astype(F32).astype(BF16)
        cl_ = cell[:, lanes]
        r = [res[t, :, lanes] for t in range(STEPS)]
        hi = [v.astype(BF16).astype(F32) for v in r]
        zero = jnp.zeros((1, blk), F32)
        rows = (
            hi
            + [(cl_ >> 13).astype(F32), ((cl_ >> 7) & 63).astype(F32), (cl_ & 127).astype(F32), zero, zero]
            + [a - h for a, h in zip(r, hi)]
            + [zero] * 5
        )
        payload = jnp.concatenate(rows, axis=0)
        lhs = (oh[:, None, :] * payload[None, :, :]).reshape(N_SPACE * 16, blk).astype(BF16)
        acc = acc + nt(lhs, slot)
    acc = acc.reshape(N_SPACE, 16, CAP)
    packed[...] = acc[:, :8, :] + acc[:, 8:, :]

    def channel_copy(k):
        to = (me + k) % N_SPACE
        return send(packed.at[to], arrived.at[me], a2a_s.at[k], a2a_r.at[k], to)

    def channel_start(k, carry):
        channel_copy(k).start()
        return carry

    lax.fori_loop(1, N_SPACE, channel_start, 0)
    start(forward_halo())
    arrived[me] = packed[me]

    lax.fori_loop(2, CX, zero_pads, 0)

    def zero_h(x, carry):
        for k in range(3):
            h0[k, x, :, :] = jnp.zeros((40, NZ), F32)
        return carry

    lax.fori_loop(0, CX + 4, zero_h, 0)

    def zero_gs(i, carry):
        for k in range(3):
            for xx in range(2):
                gs[0, k, i, pl.ds(20 * xx, 2), :] = jnp.zeros((2, NZ), F32)
                gs[3, k, i, pl.ds(20 * xx + 18, 2), :] = jnp.zeros((2, NZ), F32)
        return carry

    lax.fori_loop(0, CX // 2, zero_gs, 0)

    for c in loads_p:
        c.wait()

    def lame(x, rho):
        vp, ratio = cl[x], cm[x]
        vs = ratio * vp
        mu = rho * vs * vs
        cl[x] = COURANT * (rho * vp * vp - 2.0 * mu)
        cm[x] = COURANT * mu

    def params(x, carry):
        rho = cb[x]
        cb[x] = COURANT * (1.0 / rho)
        lame(x, rho)
        return carry

    lax.fori_loop(1, CX - 1, params, 0)
    for i, x in ends:
        lame(x, rho_end[i])
    for c in loads_f:
        c.wait()

    def speeds(x, carry=0):
        for y in range(0, NY, ROWS):
            def at(k, dx=0, dy=0):
                return F[k][x + dx, pl.ds(PAD + y + dy, ROWS), :]

            here = pl.ds(PAD + y, ROWS)
            b = cb[x - 1, pl.ds(y, ROWS), :]
            sxy, sxz, syz = at(SXY), at(SXZ), at(SYZ)
            vx = at(VX) + b * ((at(SXX, 1) - at(SXX)) + (sxy - at(SXY, 0, -1)) + zminus(sxz))
            vy = at(VY) + b * ((sxy - at(SXY, -1)) + (at(SYY, 0, 1) - at(SYY)) + zminus(syz))
            vz = at(VZ) + b * ((sxz - at(SXZ, -1)) + (syz - at(SYZ, 0, -1)) + zplus(at(SZZ)))
            F[VX][x, here, :] = vx
            F[VY][x, here, :] = vy
            F[VZ][x, here, :] = vz
        return carry

    def stresses(step, x, carry=0, add=False):
        for y in range(0, NY, ROWS):
            def at(k, dx=0, dy=0):
                return F[k][x + dx, pl.ds(PAD + y + dy, ROWS), :]

            here = pl.ds(PAD + y, ROWS)
            flat = pl.ds(y, ROWS)
            lam, mu = cl[x - 1, flat, :], cm[x - 1, flat, :]
            vx, vy, vz = at(VX), at(VY), at(VZ)
            exx = vx - at(VX, -1)
            eyy = vy - at(VY, 0, -1)
            ezz = zminus(vz)
            base = lam * (exx + eyy + ezz)
            mu2 = mu + mu
            szz = at(SZZ) + (base + mu2 * ezz)
            new = [
                at(SXX) + (base + mu2 * exx),
                at(SYY) + (base + mu2 * eyy),
                szz + dense[step, x - 1, flat, :] if step > 0 else szz,
                at(SXY) + mu * ((at(VY, 1) - vy) + (at(VX, 0, 1) - vx)),
                at(SXZ) + mu * ((at(VZ, 1) - vz) + zplus(vx)),
                at(SYZ) + mu * ((at(VZ, 0, 1) - vz) + zplus(vy)),
            ]
            for k, v in zip((SXX, SYY, SZZ, SXY, SXZ, SYZ), new):
                F[k][x, here, :] = v
            if add:
                add_terms(step, x, y, vx, vy, vz, *new)
        return carry

    def add_terms(step, x, y, vx, vy, vz, sxx, syy, szz, sxy, sxz, syz):
        def u(k, dx=0, dy=0):
            return fw[step, k, x + dx, pl.ds(PAD + y + dy, ROWS), :]

        def w(k):
            return fw[step + 1, k, x, pl.ds(PAD + y, ROWS), :]

        flat = pl.ds(y, ROWS)
        ux, uy, uz = u(0), u(1), u(2)
        fxx = ux - u(0, -1)
        fyy = uy - u(1, 0, -1)
        fzz = zminus(uz)
        lam = (fxx + fyy + fzz) * (sxx + syy + szz)
        mu = (
            2.0 * (fxx * sxx + fyy * syy + fzz * szz)
            + ((u(1, 1) - uy) + (u(0, 0, 1) - ux)) * sxy
            + ((u(2, 1) - uz) + zplus(ux)) * sxz
            + ((u(2, 0, 1) - uz) + zplus(uy)) * syz
        )
        rho = vx * (w(0) - ux) + vy * (w(1) - uy) + vz * (w(2) - uz)
        for ref, term in zip(G, (lam, mu, rho)):
            ref[x - 1, flat, :] = term if step == 0 else ref[x - 1, flat, :] + term

    def gradients(step, x, carry=0):
        for y in range(0, NY, ROWS):
            add_terms(step, x, y, *[F[k][x, pl.ds(PAD + y, ROWS), :] for k in range(9)])
        return carry

    def tile(v):
        return jnp.broadcast_to(v, (16, CAP)).astype(BF16)

    def values(s, steps):
        row = arrived[s]
        zone = (row[5:6].astype(I32) == lax.broadcasted_iota(I32, (NZ, CAP), 0)).astype(F32).astype(BF16)
        zone = zone.reshape(NZ // 16, 16, CAP)
        for t in steps:
            v = row[t : t + 1]
            hi = v.astype(BF16).astype(F32)
            b_one[t, s, pl.ds(0, NZ), :] = (zone * tile(hi)[None]).reshape(NZ, CAP)
            b_one[t, s, pl.ds(NZ, NZ), :] = (zone * tile(v - hi)[None]).reshape(NZ, CAP)

    def densify():
        def channel_wait(k, carry):
            channel_copy(k).wait_recv()
            return carry

        lax.fori_loop(1, N_SPACE, channel_wait, 0)

        def one_hot(s, carry):
            row = arrived[s]
            x, y = row[3:4].astype(I32), row[4:5].astype(I32)
            yone = (y == lax.broadcasted_iota(I32, (NY, CAP), 0)).astype(F32).astype(BF16)
            yone = yone.reshape(NY // 16, 16, CAP)
            for i in range(CX):
                xone = tile((x == i).astype(F32))
                a_one[s, pl.ds(i * NY, NY), :] = (yone * xone[None]).reshape(NY, CAP)
            values(s, (0,))
            return carry

        lax.fori_loop(0, N_SPACE, one_hot, 0)

    def product(m, t):
        rows = pl.ds(pl.multiple_of(m * 256, 256), 256)
        got = nt(
            jnp.concatenate([a_one[s, rows, :] for s in range(N_SPACE)], axis=1),
            jnp.concatenate([b_one[t, s] for s in range(N_SPACE)], axis=1),
        )
        dense[t, pl.ds(4 * m, 4), :, :] = (got[:, :NZ] + got[:, NZ:]).reshape(4, NY, NZ)

    def first_product(m, carry):
        for i in range(N_SPACE // 4):
            values(N_SPACE // 4 * m + i, (1, 2))
        product(m, 0)
        for i in range(4):
            x = 4 * m + i + 1
            F[SZZ][x, inner, :] = F[SZZ][x, inner, :] + dense[0, x - 1]
        return carry

    def later_products(m, carry):
        for t in range(1, STEPS):
            product(m, t)
        for i in range(4):
            gradients(0, 4 * m + i + 1)
        for i in range(3):
            speeds(3 * m + i + 2)
        return carry

    def end_planes(step):
        edges_in(step)
        speeds(1)
        speeds(CX)

    lax.fori_loop(2, CX, speeds, 0)
    lax.fori_loop(3, CX - 1, functools.partial(stresses, 0), 0)
    wait_recv(edge_halo(0))
    wait_recv(density_halo())
    for i in range(2):
        @pl.when(has_left if i == 0 else has_right)
        def _():
            edge_b[i] = COURANT * (1.0 / edge_b[i])
    end_planes(0)
    for x in (1, 2, CX - 1, CX):
        stresses(0, x)
    densify()
    lax.fori_loop(0, 4, first_product, 0)
    edges_out(1)
    start(edge_halo(1))
    for c in loads_w:
        c.wait()
    wait_recv(forward_halo())
    lax.fori_loop(0, 4, later_products, 0)

    def planes(first, stop, body):
        lax.fori_loop(first, stop, body, 0)

    both = [functools.partial(stresses, t, add=True) for t in range(STEPS)]
    wait_recv(edge_halo(1))
    edges_in(1)
    for x in (1, CX - 1, CX):
        speeds(x)
    stresses(1, 1)
    stresses(1, CX)
    edges_out(2)
    start(edge_halo(2))
    speeds(CX - 2)
    gradients(1, 1)
    gradients(1, CX)
    low, high = 2 * GROUPS[0][0] + 1, 2 * (GROUPS[0][0] + GROUPS[0][1]) + 1
    planes(low - 2, high + 2, both[1])
    planes(low - 1, high + 1, speeds)

    def to_mate(n):
        pairs = pl.ds(*GROUPS[n])
        return [
            pltpu.make_async_remote_copy(
                src_ref=gs.at[2 * j + 1 - core, :, pairs],
                dst_ref=rb1.at[j, :, pairs],
                send_sem=r1_s.at[n, j],
                recv_sem=r1_r.at[n, j],
                device_id={"shot": mate},
                device_id_type=pl.DeviceIdType.MESH,
            )
            for j in range(2)
        ]

    def to_cross(n):
        pairs = pl.ds(*GROUPS[n])
        return pltpu.make_async_remote_copy(
            src_ref=s2.at[:, pairs],
            dst_ref=rb2.at[:, pairs],
            send_sem=r2_s.at[n],
            recv_sem=r2_r.at[n],
            device_id={"shot": cross},
            device_id_type=pl.DeviceIdType.MESH,
        )

    def pairs_of(n, body):
        first, count = GROUPS[n]
        lax.fori_loop(first, first + count, body, 0)

    def slabs(i, carry):
        for k in range(3):
            for xx in range(2):
                for s in range(4):
                    lo, hi = max(0, 16 * s - 2), min(NY, 16 * s + 18)
                    off = 20 * xx + lo - (16 * s - 2)
                    gs[s, k, i, pl.ds(off, hi - lo), :] = G[k][2 * i + xx, pl.ds(lo, hi - lo), :]
        return carry

    def sum_cross(i, carry):
        for k in range(3):
            s2[k, i] = gs[2 * (1 - chip) + core, k, i] + rb1[1 - chip, k, i]
        return carry

    def pass_on(n):
        for c in to_mate(n):
            c.wait_recv()
        pairs_of(n, sum_cross)
        to_cross(n).start()

    for n, (first, count) in enumerate(GROUPS):
        planes(2 * first + 1, 2 * (first + count) + 1, both[2])
        pairs_of(n, slabs)
        for c in to_mate(n):
            c.start()
        if n == 0:
            planes(2, low - 2, both[1])
            planes(high + 2, CX, both[1])
            pass_on(0)
            planes(2, low - 1, speeds)
            planes(high + 1, CX, speeds)
            wait_recv(edge_halo(2))
            edges_in(2)
            speeds(1)
            speeds(CX)
        elif n > 1:
            pass_on(n - 1)
    pass_on(len(GROUPS) - 1)

    def sum_own(i, carry):
        for k in range(3):
            for xx in range(2):
                part = pl.ds(20 * xx, 20)
                total = (gs[2 * chip + core, k, i, part, :] + rb1[chip, k, i, part, :]) + rb2[k, i, part, :]
                h0[k, 2 + 2 * i + xx, pl.ds(8, 20), :] = total
        return carry

    rim = pl.ds(8, 24)
    grad_halo = (
        [send(h0.at[:, pl.ds(2, 2), rim], h0.at[:, pl.ds(CX + 2, 2), rim], gx_s.at[0], gx_r.at[0], left)],
        [send(h0.at[:, pl.ds(CX, 2), rim], h0.at[:, pl.ds(0, 2), rim], gx_s.at[1], gx_r.at[1], right)],
    )
    def sweep_one(p, carry):
        gx = CX * me + p - 2
        gy = 16 * sh - 2 + lax.broadcasted_iota(I32, (24, NZ), 0)
        keep = (gy >= 0) & (gy < NY) & (gx >= 0) & (gx < NX)
        for k in range(3):
            h1[k, p, rim, :] = jnp.where(keep, near(h0, k, p, 8, 24), 0.0)
        return carry

    for n in range(len(GROUPS)):
        to_cross(n).wait_recv()
        pairs_of(n, sum_own)
        if n == 2:
            start(grad_halo)
        if n == 3:
            planes(3, 11, sweep_one)
        if n == 4:
            planes(11, CX + 1, sweep_one)
    wait_recv(grad_halo)
    planes(1, 3, sweep_one)
    planes(CX + 1, CX + 3, sweep_one)
    wait_send(grad_halo)

    for step in range(STEPS):
        wait_send(edge_halo(step))
    wait_send(density_halo())
    wait_send(forward_halo())

    def channel_sent(k, carry):
        channel_copy(k).wait_send()
        return carry

    lax.fori_loop(1, N_SPACE, channel_sent, 0)
    for n in range(len(GROUPS)):
        for c in to_mate(n):
            c.wait_send()
        to_cross(n).wait_send()


def finish(f0, f1, f2, f3, f4, f5, f6, f7, f8, h1, out_adj, out_grad, og, sem):
    fields = (f0, f1, f2, f3, f4, f5, f6, f7, f8)
    stores = [pltpu.make_async_copy(f.at[pl.ds(1, CX), pl.ds(PAD, NY)], out_adj.at[0, k], sem.at[k]) for k, f in enumerate(fields)]
    for c in stores:
        c.start()

    def sweep_two(x, carry):
        for k in range(3):
            og[k, x] = near(h1, k, x + 2, 10, 16)
        return carry

    half = CX // 2
    parts = []
    for i in range(2):
        lax.fori_loop(half * i, half * (i + 1), sweep_two, 0)
        part = pl.ds(half * i, half)
        parts.append(pltpu.make_async_copy(og.at[:, part], out_grad.at[:, part], sem.at[9 + i]))
        parts[i].start()
    for c in parts:
        c.wait()
    for c in stores:
        c.wait()


def local(adjoint_state, forward_velocity, vp, shear_ratio, density, residuals, owner, cell):
    res = residuals.reshape(STEPS, 1, CH_DEV)
    own = owner.reshape(1, CH_DEV)
    cells = cell.reshape(1, CH_DEV)
    hbm = pl.BlockSpec(memory_space=pltpu.HBM)
    vmem = pl.BlockSpec(memory_space=pltpu.VMEM)
    volume = pltpu.VMEM((CX, NY, NZ), F32)
    dma = pltpu.SemaphoreType.DMA
    edges = pltpu.VMEM((STEPS, 3, NY, NZ), F32)
    pair = pltpu.VMEM((2, NY, NZ), F32)
    count = len(GROUPS)
    scratch = (
        [
            pltpu.VMEM((STEPS + 1, 3, CX + 2, PY, NZ), F32),
            pltpu.VMEM((STEPS, CX, NY, NZ), F32),
        ]
        + [volume] * 6
        + [edges] * 4
        + [pair] * 2
        + [
            pltpu.VMEM((STEPS, 1, CH_DEV), F32),
            pltpu.VMEM((1, CH_DEV), I32),
            pltpu.VMEM((1, CH_DEV), I32),
            pltpu.VMEM((N_SPACE, 8, CAP), F32),
            pltpu.VMEM((N_SPACE, 8, CAP), F32),
            pltpu.VMEM((N_SPACE, CX * NY, CAP), BF16),
            pltpu.VMEM((STEPS, N_SPACE, 2 * NZ, CAP), BF16),
            pltpu.VMEM((4, 3, CX // 2, 40, NZ), F32),
            pltpu.VMEM((2, 3, CX // 2, 40, NZ), F32),
            pltpu.VMEM((3, CX // 2, 40, NZ), F32),
            pltpu.VMEM((3, CX // 2, 40, NZ), F32),
            pltpu.VMEM((3, CX + 4, 40, NZ), F32),
        ]
        + [dma((9,)), dma((4,)), dma((3,)), dma((10, 2)), dma((3,))]
        + [dma((STEPS, 2)), dma((STEPS, 2)), dma((2,)), dma((2,)), dma((2,)), dma((2,)), dma((N_SPACE,)), dma((N_SPACE,))]
        + [dma((count, 2)), dma((count, 2)), dma((count,)), dma((count,)), dma((2,)), dma((2,))]
    )
    held = [(CX + 2, PY, NZ)] * 9 + [(3, CX + 4, 40, NZ)]
    given = (adjoint_state, forward_velocity, vp, shear_ratio, density, res, own, cells)
    given = [pltpu.with_memory_space_constraint(a, pltpu.HBM) for a in given]
    kept = pl.pallas_call(
        kernel,
        out_shape=tuple(pltpu.VMEM(shape, F32) for shape in held),
        in_specs=[hbm] * 8,
        out_specs=(vmem,) * len(held),
        scratch_shapes=scratch,
        compiler_params=pltpu.CompilerParams(collective_id=0, has_side_effects=True, vmem_limit_bytes=44 * 1024 * 1024),
    )(*given)
    kept = [pltpu.with_memory_space_constraint(a, pltpu.VMEM) for a in kept]
    return pl.pallas_call(
        finish,
        out_shape=(
            jax.ShapeDtypeStruct((1, 9, CX, NY, NZ), F32),
            jax.ShapeDtypeStruct((3, CX, 16, NZ), F32),
        ),
        in_specs=[vmem] * len(held),
        out_specs=(hbm, hbm),
        scratch_shapes=[pltpu.VMEM((3, CX, 16, NZ), F32), dma((11,))],
        compiler_params=pltpu.CompilerParams(vmem_limit_bytes=8 * 1024 * 1024),
    )(*kept)


def solution(mesh):
    in_specs = (
        P("shot", None, "space", None, None),
        P("shot", None, None, "space", None, None),
        P("space", None, None),
        P("space", None, None),
        P("space", None, None),
        P("shot", None, "space"),
        P("space", None),
        P("space"),
    )
    out_specs = (P("shot", None, "space", None, None), P(None, "space", "shot", None))
    return jax.shard_map(local, mesh=mesh, in_specs=in_specs, out_specs=out_specs, check_vma=False)
```
